256 devices in a mesh: dp: 8 (over z), seq: 32 (over y, x, core).
Axes of the slice: x: 4, y: 4, z: 8, core: 2. Of those that a mesh axis runs over, the one named last changes fastest.
Arguments:
- query_tiles: bfloat16 [8, 32, 128, 2048], P('dp', 'seq'), may hold values from -20 to 20
- key_tiles: bfloat16 [8, 32, 128, 2048], P('dp', 'seq'), may hold values from -6 to 6
- value_tiles: bfloat16 [8, 32, 128, 2048], P('dp', 'seq'), may hold values from -6 to 6
- attn_grad: bfloat16 [8, 32, 128, 2048], P('dp', 'seq'), may hold values from -6 to 6
- proj_grad: bfloat16 [8, 32, 128, 3072], P('dp', 'seq'), may hold values from -6 to 6
- neighbour: int32 [8, 32], P('dp'), may hold values from 0 to 31, as said below
Outputs:
- query_grad: bfloat16 [8, 32, 128, 2048], P('dp', 'seq')
- key_grad: bfloat16 [8, 32, 128, 2048], P('dp', 'seq')
- value_grad: bfloat16 [8, 32, 128, 2048], P('dp', 'seq')
- update: float32 [2048, 3072], P('dp', 'seq')
The draws below stay inside these ranges and needn't reach their ends.
Inputs may be any that keep to these rules, and one draw needn't show every extreme that they name: neighbour[v, t] is t - 1 or t + 1; tile 0 names tile 1, tile 1 names tile 0, tile 32 - 2 names tile 32 - 1 and tile 32 - 1 names tile 32 - 2.
All inputs are finite; a program needn't handle non-finite values.
Results may differ from the reference program's by a relative error of at most 0.024.
Values may be sent and summed in bfloat16 or wider, within the bound.
A program may use at most 128 MiB of HBM per device.

```python
import jax
import jax.numpy as jnp
from jax import lax

D = 3072
HEADS = 16
HEAD_DIM = 128
TILE = 128
NS_STEPS = 5
HD = 2048
VIDEOS = 8
TILES = 32


def draw_query_tiles(key, part):
    key = jax.random.fold_in(key, 11)
    first = jax.random.fold_in(key, 0)
    shape = (VIDEOS, TILES, TILE, HEADS * HEAD_DIM)
    result = jnp.clip(jax.random.normal(first, shape, jnp.float32), -6.0, 6.0)
    return result.astype(jnp.bfloat16)


def draw_key_tiles(key, part):
    key = jax.random.fold_in(key, 23)
    first = jax.random.fold_in(key, 0)
    shape = (VIDEOS, TILES, TILE, HEADS * HEAD_DIM)
    result = jnp.clip(jax.random.normal(first, shape, jnp.float32), -6.0, 6.0)
    return result.astype(jnp.bfloat16)


def draw_neighbour(key, part):
    key = jax.random.fold_in(key, 5)
    side = jax.random.randint(key, (VIDEOS, TILES), 0, 2)
    tile_ids = jnp.arange(TILES, dtype=jnp.int32)[None, :]
    target = tile_ids - 1 + 2 * side
    target = jnp.where(tile_ids == 1, 0, target)
    target = jnp.where(tile_ids == TILES - 2, TILES - 1, target)
    target = jnp.where(tile_ids == 0, 1, target)
    target = jnp.where(tile_ids == TILES - 1, TILES - 2, target)
    return target.astype(jnp.int32)


def spiked(values, own_key, source, target, parts, factor):
    owner, partner = [(jnp.arange(values.shape[position]) // (values.shape[position] // parts)).reshape([-1 if axis == position else 1 for axis in range(values.ndim)]) for position in (source, target)]
    chosen = jax.random.permutation(own_key, parts)[partner]
    strong = (owner == chosen) | (owner == (partner + parts // 2) % parts)
    return jnp.where(strong, factor * values, values)


def block_scale(own_key, shape, cuts, smallest, top_value):
    loudness = 1.0
    for position, blocks in cuts:
        heights = jax.random.uniform(jax.random.fold_in(jax.random.fold_in(own_key, 6), position), (blocks,), jnp.float32, smallest / len(cuts), top_value / len(cuts))
        loudness = loudness * jnp.repeat(jnp.exp(heights), shape[position] // blocks).reshape((-1,) + (1,) * (len(shape) - 1 - position))
    return loudness


def scatter_about(own_key, dims, spread, limit, cuts=(), kind=jnp.bfloat16):
    values = spread * jax.random.normal(own_key, dims, jnp.float32)
    if cuts:
        values = values * block_scale(own_key, dims, cuts, -0.22, 0.18)
    return jnp.clip(values, -limit, limit).astype(kind)


def gaussian_with(stream_key, shape, deviation, reach, cuts, heavy, kind=jnp.bfloat16):
    entries = deviation * jax.random.normal(stream_key, shape, jnp.float32)
    if cuts:
        entries = entries * block_scale(stream_key, shape, cuts, -0.22, 0.18)
    return jnp.clip(spiked(entries, jax.random.fold_in(stream_key, 3), *heavy), -reach, reach).astype(kind)


def setup_inputs(seed: int = 0) -> dict:
    seeds = jax.random.split(jax.random.key(seed), 7)
    query_tiles = draw_query_tiles(jax.random.fold_in(seeds[6], 71), 0)
    key_tiles = draw_key_tiles(jax.random.fold_in(seeds[6], 71), 0)
    value_tiles = scatter_about(seeds[2], (VIDEOS, TILES, TILE, HD), 1.0, 6.0, ((0, 8), (1, 32)))
    attn_grad = scatter_about(seeds[3], (VIDEOS, TILES, TILE, HD), 1.0, 6.0, ((0, 8), (1, 32)))
    proj_grad = gaussian_with(seeds[4], (VIDEOS, TILES, TILE, D), 1.0, 6.0, ((0, 8), (1, 32)), (1, 3, 32, 2.75))
    neighbour = draw_neighbour(jax.random.fold_in(seeds[6], 71), 0)
    return dict(query_tiles=query_tiles, key_tiles=key_tiles, value_tiles=value_tiles, attn_grad=attn_grad, proj_grad=proj_grad, neighbour=neighbour)


coeff_a = 3.4445
coeff_b = -4.775
coeff_c = 2.0315

def rounded(array):
    return lax.optimization_barrier(array.astype(jnp.bfloat16)).astype(jnp.float32)

def tile_grads(query_rows, key_own, value_own, key_far, value_far, out_grad):
    score_scale = HEAD_DIM ** (-0.5)
    query_h = query_rows.astype(jnp.float32).reshape(TILE, HEADS, HEAD_DIM)
    keys_all = jnp.concatenate([key_own, key_far], 0).astype(jnp.float32).reshape(2 * TILE, HEADS, HEAD_DIM)
    values_all = jnp.concatenate([value_own, value_far], 0).astype(jnp.float32).reshape(2 * TILE, HEADS, HEAD_DIM)
    grad_h = out_grad.astype(jnp.float32).reshape(TILE, HEADS, HEAD_DIM)
    scores = jnp.einsum('ihd,jhd->hij', query_h, keys_all) * score_scale
    row_max = lax.optimization_barrier(jnp.max(scores, axis=-1, keepdims=True))
    exp_scores = jnp.exp(scores - row_max)
    weights = exp_scores / lax.optimization_barrier(jnp.sum(exp_scores, axis=-1, keepdims=True))
    weights_b = rounded(weights)
    attended = rounded(jnp.einsum('hij,jhd->ihd', weights_b, values_all))
    row_delta = lax.optimization_barrier(jnp.sum(grad_h * attended, axis=-1)).T
    dweights = jnp.einsum('ihd,jhd->hij', grad_h, values_all)
    dscore_b = rounded(weights * (dweights - row_delta[:, :, None]))
    query_grad = jnp.einsum('hij,jhd->ihd', dscore_b, keys_all) * score_scale
    key_grad = jnp.einsum('hij,ihd->jhd', dscore_b, query_h) * score_scale
    value_grad = jnp.einsum('hij,ihd->jhd', weights_b, grad_h)
    width = HEADS * HEAD_DIM
    key_grad = key_grad.reshape(2 * TILE, width)
    value_grad = value_grad.reshape(2 * TILE, width)
    return (query_grad.reshape(TILE, width).astype(jnp.bfloat16), key_grad[:TILE], value_grad[:TILE], key_grad[TILE:].astype(jnp.bfloat16), value_grad[TILE:].astype(jnp.bfloat16), attended.reshape(TILE, width).astype(jnp.bfloat16))

def orthogonalize(grad_w):
    blocks = grad_w.reshape(HEADS, HEAD_DIM, D)
    frob_norm = jnp.sqrt(lax.optimization_barrier(jnp.sum(blocks * blocks, axis=(1, 2), keepdims=True))) + 1e-07
    iterate = blocks / frob_norm
    best = lax.Precision.HIGHEST
    for turn in range(NS_STEPS):
        gram_matrix = jnp.einsum('hid,hjd->hij', iterate, iterate, precision=best)
        polynomial = coeff_b * gram_matrix + coeff_c * jnp.einsum('hij,hjk->hik', gram_matrix, gram_matrix, precision=best)
        iterate = coeff_a * iterate + jnp.einsum('hij,hjd->hid', polynomial, iterate, precision=best)
    return (iterate * (0.2 * D ** 0.5)).reshape(HEADS * HEAD_DIM, D)

def reference(query_tiles, key_tiles, value_tiles, attn_grad, proj_grad, neighbour):
    width = HEADS * HEAD_DIM

    def advance(running, flat_index):
        pair_id = flat_index // TILES
        tile_id = flat_index % TILES
        total = jnp.zeros((width, D), jnp.float32)
        pieces = []
        for member in range(2):
            video_id = 2 * pair_id + member
            far_id = neighbour[video_id, tile_id]
            results = tile_grads(query_tiles[video_id, tile_id], key_tiles[video_id, tile_id], value_tiles[video_id, tile_id], key_tiles[video_id, far_id], value_tiles[video_id, far_id], attn_grad[video_id, tile_id])
            total = total + jnp.dot(results[5].T, proj_grad[video_id, tile_id], preferred_element_type=jnp.float32)
            pieces.append(results[:5])
        stacked = tuple((jnp.stack([pieces[0][k], pieces[1][k]]) for k in range(5)))
        return (running + rounded(total), stacked)
    start = jnp.zeros((width, D), jnp.float32)
    grad_w, outputs = lax.scan(advance, start, jnp.arange(VIDEOS // 2 * TILES, dtype=jnp.int32))
    shape = (VIDEOS, TILES, TILE, width)

    def unpair(array):
        return array.reshape(VIDEOS // 2, TILES, 2, TILE, width).transpose(0, 2, 1, 3, 4).reshape(shape)
    query_grad = unpair(outputs[0])
    key_own = unpair(outputs[1])
    value_own = unpair(outputs[2])
    key_far = unpair(outputs[3]).astype(jnp.float32)
    value_far = unpair(outputs[4]).astype(jnp.float32)
    tile_ids = jnp.arange(TILES, dtype=jnp.int32)[None, :]
    from_left = jnp.concatenate([jnp.zeros((VIDEOS, 1), bool), neighbour[:, :-1] == tile_ids[:, 1:]], 1)
    from_right = jnp.concatenate([neighbour[:, 1:] == tile_ids[:, :-1], jnp.zeros((VIDEOS, 1), bool)], 1)
    left_mask = from_left[:, :, None, None]
    right_mask = from_right[:, :, None, None]
    zeros_tile = jnp.zeros((VIDEOS, 1, TILE, width), jnp.float32)

    def combine(own, far):
        previous = jnp.concatenate([zeros_tile, far[:, :-1]], 1)
        following = jnp.concatenate([far[:, 1:], zeros_tile], 1)
        total = own + jnp.where(left_mask, previous, 0.0) + jnp.where(right_mask, following, 0.0)
        return total.astype(jnp.bfloat16)
    key_grad = combine(key_own, key_far)
    value_grad = combine(value_own, value_far)
    return (query_grad, key_grad, value_grad, orthogonalize(grad_w))
```

```python
import functools

import jax
import jax.numpy as jnp
from jax import lax
from jax.experimental import pallas as pl
from jax.experimental.pallas import tpu as pltpu
from jax.sharding import PartitionSpec as P

D = 3072
HEAD_DIM = 128
NS_STEPS = 5
MESH = pl.DeviceIdType.MESH
F32 = jnp.float32
BF16 = jnp.bfloat16
BEST = lax.Precision.HIGHEST

coeff_a = 3.4445
coeff_b = -4.775
coeff_c = 2.0315

NT = (((1,), (1,)), ((), ()))
NN = (((1,), (0,)), ((), ()))
TN = (((0,), (0,)), ((), ()))


def mm(a, b, dims):
    return lax.dot_general(a, b, dims, preferred_element_type=F32)


def mmh(a, b, dims=NN):
    return lax.dot_general(a, b, dims, precision=BEST, preferred_element_type=F32)


def head_grads(q, kk, vv, do):
    score_scale = HEAD_DIM ** (-0.5)
    scores = mm(q, kk, NT) * score_scale
    row_max = jnp.max(scores, axis=1, keepdims=True)
    exp_scores = jnp.exp(scores - row_max)
    weights = exp_scores / jnp.sum(exp_scores, axis=1, keepdims=True)
    weights_b = weights.astype(BF16)
    attended = mm(weights_b, vv, NN).astype(BF16)
    delta = jnp.sum(do.astype(F32) * attended.astype(F32), axis=1, keepdims=True)
    dweights = mm(do, vv, NT)
    dscore_b = (weights * (dweights - delta)).astype(BF16)
    dq = (mm(dscore_b, kk, NN) * score_scale).astype(BF16)
    dk = mm(dscore_b, q, TN) * score_scale
    dv = mm(weights_b, do, TN)
    return dq, dk, dv, attended


def kernel(
    geo,
    flags,
    q_hbm, k_hbm, v_hbm, do_hbm, proj_hbm,
    dq_ref, dk_ref, dv_ref, upd_ref,
    q_v, k_v, v_v, do_v,
    halo, far_out, far_in, own_k, own_v,
    proj_all, proj_t, att, part, rx, xsum, rz,
    g_part, g_in, g_full,
    in_sem,
    halo_s, halo_r, far_s, far_r,
    proj_s, proj_r, fwd_s, fwd_r,
    att_s, att_r, x_s, x_r, z_s, z_r,
    g1_s, g1_r, g2_s, g2_r,
):
    nz, ny, nx = geo
    seq = ny * nx * 2
    half_count = nz // 2
    tile = q_v.shape[0]
    cb = 2 * HEAD_DIM
    qcols = proj_all.shape[2]
    xcols = qcols // nx
    ccols = xcols // 2
    z = lax.axis_index("dp")
    s = lax.axis_index("seq")
    c = lax.rem(s, 2)
    x = lax.rem(s // 2, nx)
    y = s // (2 * nx)
    right = (z, lax.rem(s + 1, seq))
    left = (z, lax.rem(s + seq - 1, seq))

    def at(yy, xx, cc):
        return (z, (yy * nx + xx) * 2 + cc)

    def block_of(core, i, e):
        half = lax.rem(core + e, 2)
        return half * half_count + lax.rem(z + i, half_count)

    def lanes(block):
        return pl.ds(pl.multiple_of(block * cb, cb), cb)

    def remote(src, dst, ss, rs, dev):
        return pltpu.make_async_remote_copy(
            src_ref=src, dst_ref=dst, send_sem=ss, recv_sem=rs,
            device_id=dev, device_id_type=MESH,
        )

    own_cols = pl.ds(pl.multiple_of(y * qcols, qcols), qcols)
    loads = [
        pltpu.make_async_copy(q_hbm, q_v, in_sem.at[0]),
        pltpu.make_async_copy(k_hbm, k_v, in_sem.at[1]),
        pltpu.make_async_copy(v_hbm, v_v, in_sem.at[2]),
        pltpu.make_async_copy(do_hbm, do_v, in_sem.at[3]),
        pltpu.make_async_copy(proj_hbm.at[:, own_cols], proj_all.at[0], in_sem.at[4]),
    ]
    for load in loads:
        load.start()

    barrier = pltpu.get_barrier_semaphore()

    def greet_seq(r, carry):
        pl.semaphore_signal(
            barrier, inc=1, device_id=(z, lax.rem(s + r, seq)), device_id_type=MESH
        )
        return carry

    def greet_z(r, carry):
        for e in range(2):
            pl.semaphore_signal(
                barrier, inc=1,
                device_id=(lax.rem(z + r, nz), s - c + e), device_id_type=MESH,
            )
        return carry

    lax.fori_loop(1, seq, greet_seq, 0)
    lax.fori_loop(1, nz, greet_z, 0)
    pl.semaphore_wait(barrier, seq - 1 + 2 * (nz - 1))

    def halo_copy(i, e, kv, way):
        t = 2 * i + e
        src = (k_hbm, v_hbm)[kv].at[:, lanes(block_of(1 - c, i, e))]
        return remote(
            src, halo.at[way, kv, t], halo_s.at[way, kv, t], halo_r.at[way, kv, t],
            (right, left)[way],
        )

    def start_halo(i, carry):
        for e in range(2):
            for kv in range(2):
                for way in range(2):
                    halo_copy(i, e, kv, way).start()
        return carry

    lax.fori_loop(0, half_count, start_halo, 0)

    def proj_copy(d):
        yy = lax.rem(y + d, ny)
        cols = pl.ds(pl.multiple_of(yy * qcols, qcols), qcols)
        return remote(
            proj_hbm.at[:, cols], proj_all.at[2 * d], proj_s.at[d], proj_r.at[d],
            at(yy, x, c),
        )

    def fwd_copy(d):
        src = proj_hbm.at[:, own_cols] if d == 0 else proj_all.at[2 * d]
        return remote(
            src, proj_all.at[2 * d + 1], fwd_s.at[d], fwd_r.at[d], at(y, x, 1 - c)
        )

    for d in range(1, ny):
        proj_copy(d).start()
    fwd_copy(0).start()
    for load in loads:
        load.wait()

    go_left = flags[0]
    go_right = flags[1]
    left_sends = flags[2]
    right_sends = flags[3]

    def att_copy(i, e, d):
        slot = 2 * d + e
        place = pl.ds(slot * tile, tile)
        dst = att.at[i, place]
        return remote(
            far_out.at[2, 2 * i + e], dst, att_s.at[i, slot], att_r.at[i, slot],
            at(lax.rem(y + d, ny), x, lax.rem(c + e, 2)),
        )

    def far_copy(i, e, kv, way):
        t = 2 * i + e
        return remote(
            far_out.at[kv, t], far_in.at[way, kv, t], far_s.at[way, kv, t],
            far_r.at[way, kv, t], (right, left)[way],
        )

    def attend(i, carry):
        for e in range(2):
            t = 2 * i + e
            block = block_of(c, i, e)
            for kv in range(2):
                for way in range(2):
                    halo_copy(i, e, kv, way).wait_recv()
            for h in range(2):
                inside = pl.ds(h * HEAD_DIM, HEAD_DIM)
                cols = pl.ds(
                    pl.multiple_of(block * cb + h * HEAD_DIM, HEAD_DIM), HEAD_DIM
                )

                def beside(kv):
                    from_left = halo[0, kv, t, :, inside].astype(F32) * go_left
                    from_right = halo[1, kv, t, :, inside].astype(F32) * go_right
                    return (from_left + from_right).astype(BF16)

                q = q_v[:, cols]
                do = do_v[:, cols]
                kk = jnp.concatenate([k_v[:, cols], beside(0)], 0)
                vv = jnp.concatenate([v_v[:, cols], beside(1)], 0)
                dq, dk, dv, attended = head_grads(q, kk, vv, do)
                dq_ref[:, cols] = dq
                own_k[:, cols] = dk[:tile]
                own_v[:, cols] = dv[:tile]
                far_out[0, t, :, inside] = dk[tile:].astype(BF16)
                far_out[1, t, :, inside] = dv[tile:].astype(BF16)
                far_out[2, t, :, inside] = attended
            if e == 0:
                att[i, pl.ds(0, tile)] = far_out[2, t]
            for d in range(e == 0, ny):
                att_copy(i, e, d).start()
            for kv in range(2):
                for way in range(2):
                    far_copy(i, e, kv, way).start()
        return carry

    lax.fori_loop(0, half_count, attend, 0)

    for d in range(1, ny):
        proj_copy(d).wait_recv()
        fwd_copy(d).start()

    def turn(slot):
        proj_t[:, slot * tile : (slot + 1) * tile] = proj_all[slot].T

    for d in range(ny):
        turn(2 * d)
    for d in range(ny):
        fwd_copy(d).wait_recv()
        turn(2 * d + 1)

    def x_copy(i, d):
        xx = lax.rem(x + d, nx)
        rows = pl.ds(pl.multiple_of(xx * xcols, xcols), xcols)
        return remote(
            part.at[i, rows], rx.at[i, d], x_s.at[i, d], x_r.at[i, d], at(y, xx, c)
        )

    def z_copy(i, e):
        zz = block_of(c, i, 0)
        cc = lax.rem(c + e, 2)
        rows = pl.ds(pl.multiple_of(cc * ccols, ccols), ccols)
        slot = lax.rem(zz - z + nz, nz)
        return remote(
            xsum.at[i, rows], rz.at[slot], z_s.at[i, e], z_r.at[slot],
            (zz, s - c + cc),
        )

    def product(i):
        for d in range(ny):
            for e in range(2):
                if d + e > 0:
                    att_copy(i, e, d).wait_recv()
        part[i] = mm(proj_t[...], att[i], NN).astype(BF16)
        for d in range(1, nx):
            x_copy(i, d).start()

    def add_x(i):
        mine = pl.ds(pl.multiple_of(x * xcols, xcols), xcols)
        total = part[i, mine].astype(F32)
        for d in range(1, nx):
            x_copy(i, d).wait_recv()
            total = total + rx[i, d].astype(F32)
        xsum[i] = total.astype(BF16)
        zz = block_of(c, i, 0)

        @pl.when(zz == z)
        def _():
            rz[0] = xsum[i, pl.ds(pl.multiple_of(c * ccols, ccols), ccols)]

        @pl.when(zz != z)
        def _():
            z_copy(i, 0).start()

        z_copy(i, 1).start()

    def step(i, carry):
        @pl.when(i < half_count)
        def _():
            product(i)

        @pl.when(i > 0)
        def _():
            add_x(i - 1)

        return carry

    lax.fori_loop(0, half_count + 1, step, 0)

    def gather_far(i, carry):
        for e in range(2):
            t = 2 * i + e
            cols = lanes(block_of(1 - c, i, e))
            for kv in range(2):
                for way in range(2):
                    far_copy(i, e, kv, way).wait_recv()
                own = (own_k, own_v)[kv][:, cols]
                out = (dk_ref, dv_ref)[kv]
                out[:, cols] = (
                    own
                    + far_in[0, kv, t].astype(F32) * left_sends
                    + far_in[1, kv, t].astype(F32) * right_sends
                ).astype(BF16)
        return carry

    lax.fori_loop(0, half_count, gather_far, 0)

    def rz_copy(slot):
        return remote(rz.at[slot], rz.at[slot], z_s.at[0, 1], z_r.at[slot], right)

    @pl.when(c != z // half_count)
    def _():
        rz_copy(0).wait_recv()

    grad = rz[0].astype(F32)
    for slot in range(1, nz):
        rz_copy(slot).wait_recv()
        grad = grad + rz[slot].astype(F32)

    piece = cb // seq
    for h in range(2):
        part_h = grad[:, h * HEAD_DIM : (h + 1) * HEAD_DIM]
        g_part[h * HEAD_DIM : (h + 1) * HEAD_DIM] = mmh(part_h, part_h, TN)

    def rows_of(index):
        return pl.ds(pl.multiple_of(index * piece, piece), piece)

    def g1_copy(r):
        other = lax.rem(s + r, seq)
        return remote(
            g_part.at[rows_of(other)], g_in.at[r], g1_s.at[r], g1_r.at[r], (z, other)
        )

    def g2_copy(r):
        other = lax.rem(s + r, seq)
        return remote(
            g_full.at[rows_of(s)], g_full.at[rows_of(s)], g2_s.at[r], g2_r.at[r],
            (z, other),
        )

    def g2_from(r):
        source = rows_of(lax.rem(s + seq - r, seq))
        return remote(
            g_full.at[source], g_full.at[source], g2_s.at[r], g2_r.at[r], right
        )

    def loop(body):
        def run(r, carry):
            body(r)
            return carry

        lax.fori_loop(1, seq, run, 0)

    loop(lambda r: g1_copy(r).start())

    def add_g(r, total):
        g1_copy(r).wait_recv()
        return total + g_in[r]

    g_full[rows_of(s)] = lax.fori_loop(1, seq, add_g, g_part[rows_of(s)])
    loop(lambda r: g2_copy(r).start())
    loop(lambda r: g2_from(r).wait_recv())

    row_id = lax.broadcasted_iota(jnp.int32, (HEAD_DIM, HEAD_DIM), 0)
    col_id = lax.broadcasted_iota(jnp.int32, (HEAD_DIM, HEAD_DIM), 1)
    eye = jnp.where(row_id == col_id, 1.0, 0.0).astype(F32)
    gram, norm, whole = [], [], [None, None]
    for h in range(2):
        g = g_full[h * HEAD_DIM : (h + 1) * HEAD_DIM]
        trace = jnp.sum(jnp.sum(g * eye, axis=1, keepdims=True), axis=0, keepdims=True)
        n = jnp.sqrt(trace) + 1e-07
        norm.append(n)
        gram.append(g / n / n)
    for turn_id in range(NS_STEPS):
        square = [mmh(g, g) for g in gram]
        poly = [
            coeff_a * eye + coeff_b * g + coeff_c * g2 for g, g2 in zip(gram, square)
        ]
        if turn_id < NS_STEPS - 1:
            half_way = [mmh(p, g) for p, g in zip(poly, gram)]
        whole = [p if w is None else mmh(p, w) for p, w in zip(poly, whole)]
        if turn_id < NS_STEPS - 1:
            gram = [mmh(t, p) for t, p in zip(half_way, poly)]
    for h in range(2):
        part_h = grad[:, h * HEAD_DIM : (h + 1) * HEAD_DIM]
        result = mmh(whole[h], part_h / norm[h], NT)
        upd_ref[h * HEAD_DIM : (h + 1) * HEAD_DIM] = result * (0.2 * D**0.5)

    def drain(i, carry):
        for e in range(2):
            for kv in range(2):
                for way in range(2):
                    halo_copy(i, e, kv, way).wait_send()
                    far_copy(i, e, kv, way).wait_send()
            for d in range(e == 0, ny):
                att_copy(i, e, d).wait_send()
        for d in range(1, nx):
            x_copy(i, d).wait_send()

        @pl.when(block_of(c, i, 0) != z)
        def _():
            z_copy(i, 0).wait_send()

        z_copy(i, 1).wait_send()
        return carry

    lax.fori_loop(0, half_count, drain, 0)
    for d in range(ny):
        if d > 0:
            proj_copy(d).wait_send()
        fwd_copy(d).wait_send()
    loop(lambda r: g1_copy(r).wait_send())
    loop(lambda r: g2_copy(r).wait_send())


def local(geo, query_tiles, key_tiles, value_tiles, attn_grad, proj_grad, neighbour):
    nz, ny, nx = geo
    seq = ny * nx * 2
    hc = nz // 2
    position = lax.axis_index("seq")
    tile, width = query_tiles.shape[2:]
    depth = proj_grad.shape[3]
    qcols = depth // ny
    xcols = qcols // nx
    cb = 2 * HEAD_DIM
    group = ny * 2
    targets = neighbour[0]
    tile_ids = lax.iota(jnp.int32, targets.shape[0])
    go_left = jnp.any((tile_ids == position) & (targets < position))
    left_sends = jnp.any((tile_ids == position - 1) & (targets == position))
    right_sends = jnp.any((tile_ids == position + 1) & (targets == position))
    flags = jnp.stack([go_left, ~go_left, left_sends, right_sends]).astype(F32)
    vm = pl.BlockSpec(memory_space=pltpu.VMEM)
    anyspec = pl.BlockSpec(memory_space=pl.ANY)
    rows = jax.ShapeDtypeStruct((tile, width), BF16)
    dma = pltpu.SemaphoreType.DMA
    out = pl.pallas_call(
        functools.partial(kernel, geo),
        out_shape=(rows, rows, rows, jax.ShapeDtypeStruct((cb, depth // seq), F32)),
        in_specs=[pl.BlockSpec(memory_space=pltpu.SMEM)] + [anyspec] * 5,
        out_specs=(vm, vm, vm, vm),
        scratch_shapes=[pltpu.VMEM((tile, width), BF16)] * 4
        + [
            pltpu.VMEM((2, 2, 2 * hc, tile, cb), BF16),
            pltpu.VMEM((3, 2 * hc, tile, cb), BF16),
            pltpu.VMEM((2, 2, 2 * hc, tile, cb), BF16),
            pltpu.VMEM((tile, width), F32),
            pltpu.VMEM((tile, width), F32),
            pltpu.VMEM((group, tile, qcols), BF16),
            pltpu.VMEM((qcols, group * tile), BF16),
            pltpu.VMEM((hc, group * tile, cb), BF16),
            pltpu.VMEM((hc, qcols, cb), BF16),
            pltpu.VMEM((hc, nx, xcols, cb), BF16),
            pltpu.VMEM((hc, xcols, cb), BF16),
            pltpu.VMEM((nz, xcols // 2, cb), BF16),
            pltpu.VMEM((cb, HEAD_DIM), F32),
            pltpu.VMEM((seq, cb // seq, HEAD_DIM), F32),
            pltpu.VMEM((cb, HEAD_DIM), F32),
            dma((5,)),
            dma((2, 2, 2 * hc)), dma((2, 2, 2 * hc)),
            dma((2, 2, 2 * hc)), dma((2, 2, 2 * hc)),
            dma((ny,)), dma((ny,)), dma((ny,)), dma((ny,)),
            dma((hc, group)), dma((hc, group)),
            dma((hc, nx)), dma((hc, nx)),
            dma((hc, 2)), dma((nz,)),
            dma((seq,)), dma((seq,)), dma((seq,)), dma((seq,)),
        ],
        compiler_params=pltpu.CompilerParams(
            collective_id=0, has_side_effects=True, vmem_limit_bytes=48 * 2**20
        ),
    )(
        flags, query_tiles[0, 0], key_tiles[0, 0], value_tiles[0, 0], attn_grad[0, 0],
        proj_grad[0, 0],
    )
    return out[0][None, None], out[1][None, None], out[2][None, None], out[3]


def solution(mesh):
    nz, seq = mesh.shape["dp"], mesh.shape["seq"]
    nx = 4 if seq == 32 else 2
    geo = (nz, seq // (2 * nx), nx)
    tiled = P("dp", "seq", None, None)
    return jax.shard_map(
        functools.partial(local, geo),
        mesh=mesh,
        in_specs=(tiled, tiled, tiled, tiled, tiled, P("dp", None)),
        out_specs=(tiled, tiled, tiled, P("dp", "seq")),
        check_vma=False,
    )
```

```python
import functools

import jax
import jax.numpy as jnp
from jax import lax
from jax.experimental import pallas as pl
from jax.experimental.pallas import tpu as pltpu
from jax.sharding import PartitionSpec as P

D = 3072
HEAD_DIM = 128
NS_STEPS = 5
MESH = pl.DeviceIdType.MESH
F32 = jnp.float32
BF16 = jnp.bfloat16
BEST = lax.Precision.HIGHEST

coeff_a = 3.4445
coeff_b = -4.775
coeff_c = 2.0315

NT = (((1,), (1,)), ((), ()))
NN = (((1,), (0,)), ((), ()))
TN = (((0,), (0,)), ((), ()))


def mm(a, b, dims):
    return lax.dot_general(a, b, dims, preferred_element_type=F32)


def mmh(a, b, dims=NN):
    return lax.dot_general(a, b, dims, precision=BEST, preferred_element_type=F32)


def head_grads(q, kk, vv, do):
    score_scale = HEAD_DIM ** (-0.5)
    scores = mm(q, kk, NT) * score_scale
    row_max = jnp.max(scores, axis=1, keepdims=True)
    exp_scores = jnp.exp(scores - row_max)
    weights = exp_scores / jnp.sum(exp_scores, axis=1, keepdims=True)
    weights_b = weights.astype(BF16)
    attended = mm(weights_b, vv, NN).astype(BF16)
    delta = jnp.sum(do.astype(F32) * attended.astype(F32), axis=1, keepdims=True)
    dweights = mm(do, vv, NT)
    dscore_b = (weights * (dweights - delta)).astype(BF16)
    dq = (mm(dscore_b, kk, NN) * score_scale).astype(BF16)
    dk = mm(dscore_b, q, TN) * score_scale
    dv = mm(weights_b, do, TN)
    return dq, dk, dv, attended


def kernel(
    geo,
    nb,
    q_hbm, k_hbm, v_hbm, do_hbm, proj_hbm,
    dq_hbm, dk_hbm, dv_hbm, upd_hbm,
    q_v, k_v, v_v, do_v,
    dq_v, dk_v, dv_v, upd_v,
    halo, far_out, far_in, own_k, own_v,
    proj_all, proj_t, att, part, rx, xsum, rz,
    g_part, g_pair, g_mine, g_in, g_full, poly_all,
    in_sem, out_sem,
    halo_s, halo_r, far_s, far_r,
    proj_s, proj_r,
    att_s, att_r, fwd_s, fwd_r, x_s, x_r, z_s, z_r,
    pair_s, pair_r, g1_s, g1_r, g2_s, g2_r,
):
    nz, ny, nx = geo
    seq = ny * nx * 2
    chips = ny * nx
    hc = nz // 2
    tile = q_v.shape[0]
    cb = 2 * HEAD_DIM
    qcols = proj_all.shape[2]
    xcols = qcols // nx
    ccols = xcols // 2
    z = lax.axis_index("dp")
    s = lax.axis_index("seq")
    c = lax.rem(s, 2)
    chip = s // 2
    x = lax.rem(chip, nx)
    y = chip // nx
    a = lax.rem(y, 2)
    b = y // 2
    zrow = z // 2
    zhalf = lax.rem(z, 2)
    right = (z, lax.rem(s + 1, seq))
    left = (z, lax.rem(s + seq - 1, seq))
    other_core = (z, chip * 2 + 1 - c)

    def at(yy, xx, cc):
        return (z, (yy * nx + xx) * 2 + cc)

    def y_off(d):
        return lax.rem(y + d, ny)

    def core_off(e):
        return 1 - c if e else c

    def block_of(i, half):
        return 2 * lax.rem(zrow + i, hc) + half

    def lanes(block):
        return pl.ds(pl.multiple_of(block * cb, cb), cb)

    def remote(src, dst, ss, rs, dev):
        return pltpu.make_async_remote_copy(
            src_ref=src, dst_ref=dst, send_sem=ss, recv_sem=rs,
            device_id=dev, device_id_type=MESH,
        )

    def quarter_cols(quarter):
        return pl.ds(pl.multiple_of(quarter * qcols, qcols), qcols)

    loads = [
        pltpu.make_async_copy(k_hbm, k_v, in_sem.at[1]),
        pltpu.make_async_copy(v_hbm, v_v, in_sem.at[2]),
        pltpu.make_async_copy(q_hbm, q_v, in_sem.at[0]),
        pltpu.make_async_copy(do_hbm, do_v, in_sem.at[3]),
        pltpu.make_async_copy(
            proj_hbm.at[:, quarter_cols(2 * b + c)], proj_all.at[0], in_sem.at[4]
        ),
    ]
    for load in loads:
        load.start()

    barrier = pltpu.get_barrier_semaphore()

    def greet(dev):
        pl.semaphore_signal(barrier, inc=1, device_id=dev, device_id_type=MESH)

    def chip_off(r):
        return lax.rem(chip + r, chips)

    for r in range(1, chips):
        greet((z, chip_off(r) * 2 + c))
    for d in range(ny):
        greet(at(y_off(d), x, 1 - c))
    greet(right)
    greet(left)
    for r in range(1, nz):
        zz = lax.rem(z + r, nz)
        greet((zz, ((2 * b + zhalf) * nx + x) * 2 + a))

    def greet_targets(step, carry):
        zz = block_of(step, a)
        for cc in range(2):
            greet((zz, ((2 * b + c) * nx + x) * 2 + cc))
        return carry

    skip = jnp.where(a == zhalf, 1, 0)
    lax.fori_loop(skip, hc, greet_targets, 0)
    pl.semaphore_wait(barrier, chips - 1 + ny + 2 + nz - 1 + 2 * (hc - skip))

    def halo_copy(i, half, kv, way):
        t = 2 * i + half
        src = (k_hbm, v_hbm)[kv].at[:, lanes(block_of(i, half))]
        return remote(
            src, halo.at[way, kv, t], halo_s.at[way, kv, t], halo_r.at[way, kv, t],
            (right, left)[way],
        )

    def start_halo(i, carry):
        for half in range(2):
            for kv in range(2):
                for way in range(2):
                    halo_copy(i, half, kv, way).start()
        return carry

    lax.fori_loop(0, hc, start_halo, 0)

    others = [(d, e) for d in range(ny) for e in range(2) if d + e > 0]

    def proj_copy(d, e):
        yy, cc = y_off(d), core_off(e)
        slot = 2 * d + e
        return remote(
            proj_hbm.at[:, quarter_cols(2 * (yy // 2) + cc)], proj_all.at[slot],
            proj_s.at[slot], proj_r.at[slot], at(yy, x, cc),
        )

    for d, e in others:
        proj_copy(d, e).start()
    for load in loads:
        load.wait()

    def mask(condition):
        return jnp.where(condition, jnp.float32(1.0), jnp.float32(0.0))

    go_left = mask(nb[0, s] < s)
    go_right = 1.0 - go_left
    left_sends = mask(nb[0, jnp.maximum(s - 1, 0)] == s)
    right_sends = mask(nb[0, jnp.minimum(s + 1, seq - 1)] == s)

    def att_copy(i, d):
        half = a if d % 2 == 0 else 1 - a
        return remote(
            far_out.at[2, 2 * i + half], att.at[i, pl.ds(2 * d * tile, tile)],
            att_s.at[i, d], att_r.at[i, d], at(y_off(d), x, c),
        )

    def fwd_copy(i, d):
        src = far_out.at[2, 2 * i + a] if d == 0 else att.at[i, pl.ds(2 * d * tile, tile)]
        return remote(
            src, att.at[i, pl.ds((2 * d + 1) * tile, tile)],
            fwd_s.at[i, d], fwd_r.at[i, d], other_core,
        )

    def far_copy(i, half, kv, way):
        t = 2 * i + half
        return remote(
            far_out.at[kv, t], far_in.at[way, kv, t], far_s.at[way, kv, t],
            far_r.at[way, kv, t], (right, left)[way],
        )

    turns_right = (x == nx - 1) & (c == 1)
    turns_left = (x == 0) & (c == 0)

    def start_far(i, half, late):
        for way in range(2):
            turns = (turns_right, turns_left)[way]

            @pl.when(turns if late else ~turns)
            def _():
                for kv in range(2):
                    far_copy(i, half, kv, way).start()

    def attend(i, carry):
        for half in range(2):
            t = 2 * i + half
            block = block_of(i, half)
            for kv in range(2):
                for way in range(2):
                    halo_copy(i, half, kv, way).wait_recv()
            for h in range(2):
                inside = pl.ds(h * HEAD_DIM, HEAD_DIM)
                cols = pl.ds(
                    pl.multiple_of(block * cb + h * HEAD_DIM, HEAD_DIM), HEAD_DIM
                )

                def beside(kv):
                    from_left = halo[0, kv, t, :, inside].astype(F32) * go_left
                    from_right = halo[1, kv, t, :, inside].astype(F32) * go_right
                    return (from_left + from_right).astype(BF16)

                q = q_v[:, cols]
                do = do_v[:, cols]
                kk = jnp.concatenate([k_v[:, cols], beside(0)], 0)
                vv = jnp.concatenate([v_v[:, cols], beside(1)], 0)
                dq, dk, dv, attended = head_grads(q, kk, vv, do)
                dq_v[:, cols] = dq
                own_k[:, cols] = dk[:tile]
                own_v[:, cols] = dv[:tile]
                far_out[0, t, :, inside] = dk[tile:].astype(BF16)
                far_out[1, t, :, inside] = dv[tile:].astype(BF16)
                far_out[2, t, :, inside] = attended

            @pl.when(a == half)
            def _():
                att[i, pl.ds(0, tile)] = far_out[2, t]
                fwd_copy(i, 0).start()

            start_far(i, half, False)
        return carry

    lax.fori_loop(0, hc, attend, 0)
    dq_out = pltpu.make_async_copy(dq_v, dq_hbm, out_sem.at[0])
    dq_out.start()

    def send_att(i):
        for d in range(1, ny):
            att_copy(i, d).start()

    ahead = 2
    for i in range(min(ahead, hc)):
        send_att(i)

    def turn(slot):
        proj_t[:, slot * tile : (slot + 1) * tile] = proj_all[slot].T

    turn(0)
    for d, e in others:
        proj_copy(d, e).wait_recv()
        turn(2 * d + e)

    def x_copy(i, d):
        xx = lax.rem(x + d, nx)
        rows = pl.ds(pl.multiple_of(xx * xcols, xcols), xcols)
        return remote(
            part.at[i, rows], rx.at[i, d], x_s.at[i, d], x_r.at[i, d], at(y, xx, c)
        )

    def z_copy(i, e):
        zz = block_of(i, a)
        cc = core_off(e)
        rows = pl.ds(pl.multiple_of(cc * ccols, ccols), ccols)
        slot = lax.rem(zz - z + nz, nz)
        return remote(
            xsum.at[i, rows], rz.at[slot], z_s.at[i, e], z_r.at[slot],
            (zz, ((2 * b + c) * nx + x) * 2 + cc),
        )

    def stays(i):
        return (block_of(i, a) == z) & (c == a)

    def forward(i):
        for d in range(1, ny):
            att_copy(i, d).wait_recv()
            fwd_copy(i, d).start()

        @pl.when(i + ahead < hc)
        def _():
            send_att(i + ahead)

    def product(i):
        for d in range(ny):
            fwd_copy(i, d).wait_recv()
        part[i] = mm(proj_t[...], att[i], NN).astype(BF16)
        for d in range(1, nx):
            x_copy(i, d).start()

    def add_x(i):
        mine = pl.ds(pl.multiple_of(x * xcols, xcols), xcols)
        total = part[i, mine].astype(F32)
        for d in range(1, nx):
            x_copy(i, d).wait_recv()
            total = total + rx[i, d].astype(F32)
        xsum[i] = total.astype(BF16)
        here = stays(i)

        @pl.when(here)
        def _():
            rz[0] = xsum[i, pl.ds(pl.multiple_of(c * ccols, ccols), ccols)]

        @pl.when(~here)
        def _():
            z_copy(i, 0).start()

        z_copy(i, 1).start()

    def step(i, carry):
        @pl.when(i < hc)
        def _():
            forward(i)

        @pl.when(i > 0)
        def _():
            product(i - 1)

        return carry

    lax.fori_loop(0, hc + 1, step, 0)

    def sums(i, carry):
        add_x(i)
        return carry

    lax.fori_loop(0, hc, sums, 0)

    def late_far(i, carry):
        for half in range(2):
            start_far(i, half, True)
        return carry

    lax.fori_loop(0, hc, late_far, 0)

    def rz_copy(slot):
        return remote(rz.at[slot], rz.at[slot], z_s.at[0, 1], z_r.at[slot], right)

    @pl.when(~((zhalf == a) & (c == a)))
    def _():
        rz_copy(0).wait_recv()

    grad = rz[0].astype(F32)
    for slot in range(1, nz):
        rz_copy(slot).wait_recv()
        grad = grad + rz[slot].astype(F32)

    piece = HEAD_DIM // chips
    for h in range(2):
        part_h = grad[:, h * HEAD_DIM : (h + 1) * HEAD_DIM]
        g_part[h] = mmh(part_h, part_h, TN)
    pair = remote(
        g_part.at[1 - c], g_pair, pair_s.at[0], pair_r.at[0], other_core
    )
    pair.start()
    pair.wait_recv()
    g_mine[...] = g_part[c] + g_pair[...]

    def rows_of(index):
        return pl.ds(pl.multiple_of(index * piece, piece), piece)

    def g1_copy(r):
        there = chip_off(r)
        return remote(
            g_mine.at[rows_of(there)], g_in.at[r], g1_s.at[r], g1_r.at[r],
            (z, there * 2 + c),
        )

    def g2_copy(r):
        return remote(
            g_full.at[rows_of(chip)], g_full.at[rows_of(chip)], g2_s.at[r],
            g2_r.at[r], (z, chip_off(r) * 2 + c),
        )

    def g2_from(r):
        source = rows_of(lax.rem(chip + chips - r, chips))
        return remote(
            g_full.at[source], g_full.at[source], g2_s.at[r], g2_r.at[r], right
        )

    for r in range(1, chips):
        g1_copy(r).start()
    total = g_mine[rows_of(chip)]
    for r in range(1, chips):
        g1_copy(r).wait_recv()
        total = total + g_in[r]
    g_full[rows_of(chip)] = total
    for r in range(1, chips):
        g2_copy(r).start()

    def gather_far(i, carry):
        for half in range(2):
            t = 2 * i + half
            cols = lanes(block_of(i, half))
            for kv in range(2):
                for way in range(2):
                    far_copy(i, half, kv, way).wait_recv()
                out = (dk_v, dv_v)[kv]
                out[:, cols] = (
                    (own_k, own_v)[kv][:, cols]
                    + far_in[0, kv, t].astype(F32) * left_sends
                    + far_in[1, kv, t].astype(F32) * right_sends
                ).astype(BF16)
        return carry

    lax.fori_loop(0, hc, gather_far, 0)
    dk_out = pltpu.make_async_copy(dk_v, dk_hbm, out_sem.at[1])
    dv_out = pltpu.make_async_copy(dv_v, dv_hbm, out_sem.at[2])
    dk_out.start()
    dv_out.start()

    for r in range(1, chips):
        g2_from(r).wait_recv()

    row_id = lax.broadcasted_iota(jnp.int32, (HEAD_DIM, HEAD_DIM), 0)
    col_id = lax.broadcasted_iota(jnp.int32, (HEAD_DIM, HEAD_DIM), 1)
    eye = jnp.where(row_id == col_id, 1.0, 0.0).astype(F32)
    gram = g_full[...]
    trace = jnp.sum(jnp.sum(gram * eye, axis=1, keepdims=True), axis=0, keepdims=True)
    norm = jnp.sqrt(trace) + 1e-07
    gram = gram / norm / norm
    whole = None
    for turn_id in range(NS_STEPS):
        poly = coeff_a * eye + coeff_b * gram + coeff_c * mmh(gram, gram)
        if turn_id < NS_STEPS - 1:
            gram = mmh(mmh(poly, gram), poly)
        whole = poly if whole is None else mmh(poly, whole)
    poly_all[c] = whole / norm
    swap = remote(
        poly_all.at[c], poly_all.at[c], pair_s.at[1], pair_r.at[1], other_core
    )
    swap.start()
    remote(
        poly_all.at[1 - c], poly_all.at[1 - c], pair_s.at[1], pair_r.at[1], other_core
    ).wait_recv()
    for h in range(2):
        part_h = grad[:, h * HEAD_DIM : (h + 1) * HEAD_DIM]
        result = mmh(part_h, poly_all[h], NT)
        upd_v[:, h * HEAD_DIM : (h + 1) * HEAD_DIM] = result * (0.2 * D**0.5)
    upd_out = pltpu.make_async_copy(upd_v, upd_hbm, out_sem.at[3])
    upd_out.start()

    def drain(i, carry):
        for half in range(2):
            for kv in range(2):
                for way in range(2):
                    halo_copy(i, half, kv, way).wait_send()
                    far_copy(i, half, kv, way).wait_send()
        for d in range(ny):
            if d > 0:
                att_copy(i, d).wait_send()
            fwd_copy(i, d).wait_send()
        for d in range(1, nx):
            x_copy(i, d).wait_send()

        @pl.when(~stays(i))
        def _():
            z_copy(i, 0).wait_send()

        z_copy(i, 1).wait_send()
        return carry

    lax.fori_loop(0, hc, drain, 0)
    for d, e in others:
        proj_copy(d, e).wait_send()
    pair.wait_send()
    swap.wait_send()
    for r in range(1, chips):
        g1_copy(r).wait_send()
        g2_copy(r).wait_send()
    for out in (dq_out, dk_out, dv_out, upd_out):
        out.wait()


def settle_kernel(*refs):
    count = (len(refs) - 2) // 3
    ins, outs, kept = refs[:count], refs[count : 2 * count], refs[2 * count : 3 * count]
    in_sem, out_sem = refs[-2:]
    loads = [
        pltpu.make_async_copy(ins[n], kept[n], in_sem.at[n]) for n in range(count)
    ]
    stores = [
        pltpu.make_async_copy(kept[n], outs[n], out_sem.at[n]) for n in range(count)
    ]
    for load in loads:
        load.start()
    for load, store in zip(loads, stores):
        load.wait()
        store.start()
    for store in stores:
        store.wait()


def settle(*arrays):
    anyspec = pl.BlockSpec(memory_space=pl.ANY)
    sems = pltpu.SemaphoreType.DMA((len(arrays),))
    return pl.pallas_call(
        settle_kernel,
        out_shape=tuple(jax.ShapeDtypeStruct(a.shape, a.dtype) for a in arrays),
        in_specs=[anyspec] * len(arrays),
        out_specs=(anyspec,) * len(arrays),
        scratch_shapes=[pltpu.VMEM(a.shape, a.dtype) for a in arrays] + [sems, sems],
        compiler_params=pltpu.CompilerParams(vmem_limit_bytes=60 * 2**20),
    )(*arrays)


def local(geo, query_tiles, key_tiles, value_tiles, attn_grad, proj_grad, neighbour):
    nz, ny, nx = geo
    seq = ny * nx * 2
    hc = nz // 2
    tile, width = query_tiles.shape[2:]
    depth = proj_grad.shape[3]
    qcols = depth // ny
    xcols = qcols // nx
    cb = 2 * HEAD_DIM
    group = ny * 2
    anyspec = pl.BlockSpec(memory_space=pl.ANY)
    chips = seq // 2
    rows = jax.ShapeDtypeStruct((tile, width), BF16)
    dma = pltpu.SemaphoreType.DMA
    halves = (2, 2, 2 * hc)
    square = (HEAD_DIM, HEAD_DIM)
    out = pl.pallas_call(
        functools.partial(kernel, geo),
        out_shape=(rows, rows, rows, jax.ShapeDtypeStruct((depth // seq, cb), F32)),
        in_specs=[pl.BlockSpec(memory_space=pltpu.SMEM)] + [anyspec] * 5,
        out_specs=(anyspec,) * 4,
        scratch_shapes=[pltpu.VMEM((tile, width), BF16)] * 7
        + [
            pltpu.VMEM((depth // seq, cb), F32),
            pltpu.VMEM(halves + (tile, cb), BF16),
            pltpu.VMEM((3, 2 * hc, tile, cb), BF16),
            pltpu.VMEM(halves + (tile, cb), BF16),
            pltpu.VMEM((tile, width), F32),
            pltpu.VMEM((tile, width), F32),
            pltpu.VMEM((group, tile, qcols), BF16),
            pltpu.VMEM((qcols, group * tile), BF16),
            pltpu.VMEM((hc, group * tile, cb), BF16),
            pltpu.VMEM((hc, qcols, cb), BF16),
            pltpu.VMEM((hc, nx, xcols, cb), BF16),
            pltpu.VMEM((hc, xcols, cb), BF16),
            pltpu.VMEM((nz, xcols // 2, cb), BF16),
            pltpu.VMEM((2,) + square, F32),
            pltpu.VMEM(square, F32),
            pltpu.VMEM(square, F32),
            pltpu.VMEM((chips, HEAD_DIM // chips, HEAD_DIM), F32),
            pltpu.VMEM(square, F32),
            pltpu.VMEM((2,) + square, F32),
            dma((5,)), dma((4,)),
            dma(halves), dma(halves), dma(halves), dma(halves),
            dma((group,)), dma((group,)),
            dma((hc, ny)), dma((hc, ny)), dma((hc, ny)), dma((hc, ny)),
            dma((hc, nx)), dma((hc, nx)), dma((hc, 2)), dma((nz,)),
            dma((2,)), dma((2,)),
            dma((chips,)), dma((chips,)), dma((chips,)), dma((chips,)),
        ],
        compiler_params=pltpu.CompilerParams(
            collective_id=0, has_side_effects=True, vmem_limit_bytes=60 * 2**20
        ),
    )(
        neighbour, query_tiles[0, 0], key_tiles[0, 0], value_tiles[0, 0],
        attn_grad[0, 0], proj_grad[0, 0],
    )
    dq, dk, dv, upd = settle(*out)
    return dq[None, None], dk[None, None], dv[None, None], upd.T


def solution(mesh):
    nz, seq = mesh.shape["dp"], mesh.shape["seq"]
    nx = 4 if seq == 32 else 2
    geo = (nz, seq // (2 * nx), nx)
    tiled = P("dp", "seq", None, None)
    return jax.shard_map(
        functools.partial(local, geo),
        mesh=mesh,
        in_specs=(tiled, tiled, tiled, tiled, tiled, P("dp", None)),
        out_specs=(tiled, tiled, tiled, P("dp", "seq")),
        check_vma=False,
    )
```

```python
import functools

import jax
import jax.numpy as jnp
from jax import lax
from jax.experimental import pallas as pl
from jax.experimental.pallas import tpu as pltpu
from jax.sharding import PartitionSpec as P

D = 3072
HEAD_DIM = 128
NS_STEPS = 5
MESH = pl.DeviceIdType.MESH
F32 = jnp.float32
BF16 = jnp.bfloat16
BEST = lax.Precision.HIGHEST

coeff_a = 3.4445
coeff_b = -4.775
coeff_c = 2.0315

NT = (((1,), (1,)), ((), ()))
NN = (((1,), (0,)), ((), ()))
TN = (((0,), (0,)), ((), ()))


def mm(a, b, dims):
    return lax.dot_general(a, b, dims, preferred_element_type=F32)


def mmh(a, b, dims=NN):
    return lax.dot_general(a, b, dims, precision=BEST, preferred_element_type=F32)


def head_grads(q, kk, vv, do):
    score_scale = HEAD_DIM ** (-0.5)
    scores = mm(q, kk, NT) * score_scale
    row_max = jnp.max(scores, axis=1, keepdims=True)
    exp_scores = jnp.exp(scores - row_max)
    weights = exp_scores / jnp.sum(exp_scores, axis=1, keepdims=True)
    weights_b = weights.astype(BF16)
    attended = mm(weights_b, vv, NN).astype(BF16)
    delta = jnp.sum(do.astype(F32) * attended.astype(F32), axis=1, keepdims=True)
    dweights = mm(do, vv, NT)
    dscore_b = (weights * (dweights - delta)).astype(BF16)
    dq = (mm(dscore_b, kk, NN) * score_scale).astype(BF16)
    dk = mm(dscore_b, q, TN) * score_scale
    dv = mm(weights_b, do, TN)
    return dq, dk, dv, attended


def kernel(
    geo,
    nb,
    q_hbm, k_hbm, v_hbm, do_hbm, proj_hbm,
    dq_hbm, dk_hbm, dv_hbm, upd_hbm,
    q_v, k_v, v_v, do_v,
    dq_v, dk_v, dv_v, upd_v,
    halo, far_out, far_in, own_k, own_v,
    proj_all, proj_t, att, part, rx1, sum1, rx2, sum2, rz,
    g_part, g_pair, g_mine, g_in, g_full, poly_all,
    in_sem, out_sem,
    halo_s, halo_r, far_s, far_r,
    proj_s, proj_r,
    att_s, att_r, s1_s, s1_r, s2_s, s2_r, z_s, z_r,
    pair_s, pair_r, g1_s, g1_r, g2_s, g2_r,
):
    nz, ny, nx = geo
    seq = ny * nx * 2
    chips = ny * nx
    hc = nz // 2
    tile = q_v.shape[0]
    cb = 2 * HEAD_DIM
    hcols = proj_all.shape[2]
    ys = ny // 2
    ccols = hcols // chips
    z = lax.axis_index("dp")
    s = lax.axis_index("seq")
    c = lax.rem(s, 2)
    chip = s // 2
    x = lax.rem(chip, nx)
    y = chip // nx
    p = lax.rem(z, 2)
    zp = z // 2
    right = (z, lax.rem(s + 1, seq))
    left = (z, lax.rem(s + seq - 1, seq))
    other_core = (z, chip * 2 + 1 - c)

    def at(yy, xx, cc):
        return (z, (yy * nx + xx) * 2 + cc)

    def mate(cc):
        return (z + 1 - 2 * p, chip * 2 + cc)

    def y_off(d):
        return lax.rem(y + d, ny)

    def block_of(i, half):
        return 2 * lax.rem(zp + i, hc) + half

    def lanes(block):
        return pl.ds(pl.multiple_of(block * cb, cb), cb)

    def remote(src, dst, ss, rs, dev):
        return pltpu.make_async_remote_copy(
            src_ref=src, dst_ref=dst, send_sem=ss, recv_sem=rs,
            device_id=dev, device_id_type=MESH,
        )

    def half_cols(half):
        return pl.ds(pl.multiple_of(half * hcols, hcols), hcols)

    loads = [
        pltpu.make_async_copy(k_hbm, k_v, in_sem.at[1]),
        pltpu.make_async_copy(v_hbm, v_v, in_sem.at[2]),
        pltpu.make_async_copy(q_hbm, q_v, in_sem.at[0]),
        pltpu.make_async_copy(do_hbm, do_v, in_sem.at[3]),
        pltpu.make_async_copy(
            proj_hbm.at[:, half_cols(p)], proj_all.at[0], in_sem.at[4]
        ),
    ]
    for load in loads:
        load.start()

    barrier = pltpu.get_barrier_semaphore()

    def greet(dev):
        pl.semaphore_signal(barrier, inc=1, device_id=dev, device_id_type=MESH)

    def chip_off(r):
        return lax.rem(chip + r, chips)

    def owner(i):
        return (block_of(i, c), (((p * ys + y // 2) * nx) + x) * 2 + lax.rem(y, 2))

    stays = (c == p) & (p * ys + y // 2 == y) & (lax.rem(y, 2) == c)

    for r in range(1, chips):
        greet((z, chip_off(r) * 2 + c))
    greet(other_core)
    greet(mate(c))
    greet(mate(1 - c))
    greet(right)
    greet(left)
    source_chip = (2 * lax.rem(y, ys) + c) * nx + x
    for m in range(1, hc):
        greet(owner(m))
        greet((2 * lax.rem(zp + m, hc) + y // ys, source_chip * 2 + p))

    @pl.when(~stays)
    def _():
        greet(owner(0))
        greet((2 * zp + y // ys, source_chip * 2 + p))

    pl.semaphore_wait(
        barrier, chips - 1 + 5 + 2 * (hc - 1) + jnp.where(stays, 0, 2)
    )

    def halo_copy(i, half, kv, way):
        t = 2 * i + half
        src = (k_hbm, v_hbm)[kv].at[:, lanes(block_of(i, half))]
        return remote(
            src, halo.at[way, kv, t], halo_s.at[way, kv, t], halo_r.at[way, kv, t],
            (right, left)[way],
        )

    def start_halo(i, carry):
        for half in range(2):
            for kv in range(2):
                for way in range(2):
                    halo_copy(i, half, kv, way).start()
        return carry

    lax.fori_loop(0, hc, start_halo, 0)

    def proj_copy(slot):
        if slot == 3:
            src = proj_all.at[2]
        else:
            src = proj_hbm.at[:, half_cols(p if slot == 1 else 1 - p)]
        return remote(
            src, proj_all.at[slot], proj_s.at[slot], proj_r.at[slot],
            mate(c) if slot == 2 else other_core,
        )

    proj_copy(2).start()
    proj_copy(1).start()
    for load in loads:
        load.wait()

    def mask(condition):
        return jnp.where(condition, jnp.float32(1.0), jnp.float32(0.0))

    go_left = mask(nb[0, s] < s)
    go_right = 1.0 - go_left
    left_sends = mask(nb[0, jnp.maximum(s - 1, 0)] == s)
    right_sends = mask(nb[0, jnp.minimum(s + 1, seq - 1)] == s)

    def att_copy(i, slot):
        half = c if slot == 2 else 1 - c
        return remote(
            far_out.at[2, 2 * i + half], att.at[i, pl.ds(slot * tile, tile)],
            att_s.at[i, slot], att_r.at[i, slot],
            (None, other_core, mate(c), mate(1 - c))[slot],
        )

    def far_copy(i, half, kv, way):
        t = 2 * i + half
        return remote(
            far_out.at[kv, t], far_in.at[way, kv, t], far_s.at[way, kv, t],
            far_r.at[way, kv, t], (right, left)[way],
        )

    def start_far(i, half):
        for way in range(2):
            for kv in range(2):
                far_copy(i, half, kv, way).start()

    def turn(slot):
        turned = proj_all[slot].T
        for yy in range(ny):
            for xx in range(nx):
                start = (((yy // 2) * nx + xx) * 2 + yy % 2) * ccols
                place = (yy * nx + xx) * ccols
                proj_t[place : place + ccols, slot * tile : (slot + 1) * tile] = turned[
                    start : start + ccols
                ]

    def turn_all():
        turn(0)
        turn(2)
        for slot in (1, 3):
            proj_copy(slot).wait_recv()
            turn(slot)

    def first_copy(i, d):
        if i % 2 == 0:
            xx = lax.rem(x + d, nx)
            src, dev = part.at[i, :, xx], at(y, xx, c)
        else:
            src, dev = part.at[i, y_off(d)], at(y_off(d), x, c)
        return remote(src, rx1.at[i, d], s1_s.at[i, d], s1_r.at[i, d], dev)

    def second_copy(i, d):
        if i % 2 == 0:
            src, dev = sum1.at[i, y_off(d)], at(y_off(d), x, c)
        else:
            xx = lax.rem(x + d, nx)
            src, dev = sum1.at[i, xx], at(y, xx, c)
        return remote(src, rx2.at[i, d], s2_s.at[i, d], s2_r.at[i, d], dev)

    def z_copy(i):
        return remote(sum2.at[i], rz.at[i], z_s.at[i], z_r.at[i], owner(i))

    def product(i):
        for slot in range(1, 4):
            att_copy(i, slot).wait_recv()
        part[i] = mm(proj_t[...], att[i], NN).astype(BF16).reshape(part.shape[1:])
        for d in range(1, nx if i % 2 == 0 else ny):
            first_copy(i, d).start()

    early = min(2, hc - 1)

    def attend(i, carry):
        if early:

            @pl.when(i == hc - 1)
            def _():
                turn_all()
                for k in range(early):
                    product(k)

        for half in range(2):
            t = 2 * i + half
            block = block_of(i, half)
            for kv in range(2):
                for way in range(2):
                    halo_copy(i, half, kv, way).wait_recv()
            for h in range(2):
                inside = pl.ds(h * HEAD_DIM, HEAD_DIM)
                cols = pl.ds(
                    pl.multiple_of(block * cb + h * HEAD_DIM, HEAD_DIM), HEAD_DIM
                )

                def beside(kv):
                    from_left = halo[0, kv, t, :, inside].astype(F32) * go_left
                    from_right = halo[1, kv, t, :, inside].astype(F32) * go_right
                    return (from_left + from_right).astype(BF16)

                q = q_v[:, cols]
                do = do_v[:, cols]
                kk = jnp.concatenate([k_v[:, cols], beside(0)], 0)
                vv = jnp.concatenate([v_v[:, cols], beside(1)], 0)
                dq, dk, dv, attended = head_grads(q, kk, vv, do)
                dq_v[:, cols] = dq
                own_k[:, cols] = dk[:tile]
                own_v[:, cols] = dv[:tile]
                far_out[0, t, :, inside] = dk[tile:].astype(BF16)
                far_out[1, t, :, inside] = dv[tile:].astype(BF16)
                far_out[2, t, :, inside] = attended

            @pl.when(c == half)
            def _():
                att_copy(i, 2).start()
                att[i, pl.ds(0, tile)] = far_out[2, t]

            @pl.when(c != half)
            def _():
                att_copy(i, 3).start()
                att_copy(i, 1).start()

        @pl.when(i == max(hc - 2, 0))
        def _():
            proj_copy(2).wait_recv()
            proj_copy(3).start()

        return carry

    lax.fori_loop(0, hc, attend, 0)
    dq_out = pltpu.make_async_copy(dq_v, dq_hbm, out_sem.at[0])
    dq_out.start()

    if not early:
        turn_all()
    for i in range(early, hc):
        product(i)
    for i in range(hc):
        total = (part[i, :, x] if i % 2 == 0 else part[i, y]).astype(F32)
        for d in range(1, nx if i % 2 == 0 else ny):
            first_copy(i, d).wait_recv()
            total = total + rx1[i, d].astype(F32)
        sum1[i] = total.astype(BF16)
        for d in range(1, ny if i % 2 == 0 else nx):
            second_copy(i, d).start()
    for i in range(hc):
        total = sum1[i, y if i % 2 == 0 else x].astype(F32)
        for d in range(1, ny if i % 2 == 0 else nx):
            second_copy(i, d).wait_recv()
            total = total + rx2[i, d].astype(F32)
        sum2[i] = total.astype(BF16)
        if i == 0:

            @pl.when(stays)
            def _():
                rz[0] = sum2[0]

            @pl.when(~stays)
            def _():
                z_copy(0).start()

        else:
            z_copy(i).start()

    def send_far(i, carry):
        for half in range(2):
            start_far(i, half)
        return carry

    lax.fori_loop(0, hc, send_far, 0)

    @pl.when(~stays)
    def _():
        z_copy(0).wait_recv()

    grad = rz[0].astype(F32)
    for i in range(1, hc):
        z_copy(i).wait_recv()
        grad = grad + rz[i].astype(F32)

    piece = HEAD_DIM // chips
    for h in range(2):
        part_h = grad[:, h * HEAD_DIM : (h + 1) * HEAD_DIM]
        g_part[h] = mmh(part_h, part_h, TN)
    pair = remote(
        g_part.at[1 - c], g_pair, pair_s.at[0], pair_r.at[0], other_core
    )
    pair.start()
    pair.wait_recv()
    g_mine[...] = g_part[c] + g_pair[...]

    def rows_of(index):
        return pl.ds(pl.multiple_of(index * piece, piece), piece)

    def g1_copy(r):
        there = chip_off(r)
        return remote(
            g_mine.at[rows_of(there)], g_in.at[r], g1_s.at[r], g1_r.at[r],
            (z, there * 2 + c),
        )

    def g2_copy(r):
        return remote(
            g_full.at[rows_of(chip)], g_full.at[rows_of(chip)], g2_s.at[r],
            g2_r.at[r], (z, chip_off(r) * 2 + c),
        )

    def g2_from(r):
        source = rows_of(lax.rem(chip + chips - r, chips))
        return remote(
            g_full.at[source], g_full.at[source], g2_s.at[r], g2_r.at[r], right
        )

    for r in range(1, chips):
        g1_copy(r).start()
    total = g_mine[rows_of(chip)]
    for r in range(1, chips):
        g1_copy(r).wait_recv()
        total = total + g_in[r]
    g_full[rows_of(chip)] = total
    for r in range(1, chips):
        g2_copy(r).start()

    def gather_far(i, carry):
        for half in range(2):
            t = 2 * i + half
            cols = lanes(block_of(i, half))
            for kv in range(2):
                for way in range(2):
                    far_copy(i, half, kv, way).wait_recv()
                out = (dk_v, dv_v)[kv]
                out[:, cols] = (
                    (own_k, own_v)[kv][:, cols]
                    + far_in[0, kv, t].astype(F32) * left_sends
                    + far_in[1, kv, t].astype(F32) * right_sends
                ).astype(BF16)
        return carry

    lax.fori_loop(0, hc, gather_far, 0)
    dk_out = pltpu.make_async_copy(dk_v, dk_hbm, out_sem.at[1])
    dv_out = pltpu.make_async_copy(dv_v, dv_hbm, out_sem.at[2])
    dk_out.start()
    dv_out.start()

    for r in range(1, chips):
        g2_from(r).wait_recv()

    row_id = lax.broadcasted_iota(jnp.int32, (HEAD_DIM, HEAD_DIM), 0)
    col_id = lax.broadcasted_iota(jnp.int32, (HEAD_DIM, HEAD_DIM), 1)
    eye = jnp.where(row_id == col_id, 1.0, 0.0).astype(F32)
    gram = g_full[...]
    trace = jnp.sum(jnp.sum(gram * eye, axis=1, keepdims=True), axis=0, keepdims=True)
    norm = jnp.sqrt(trace) + 1e-07
    gram = gram / norm / norm
    whole = None
    for turn_id in range(NS_STEPS):
        poly = coeff_a * eye + coeff_b * gram + coeff_c * mmh(gram, gram)
        if turn_id < NS_STEPS - 1:
            gram = mmh(mmh(poly, gram), poly)
        whole = poly if whole is None else mmh(poly, whole)
    poly_all[c] = whole / norm
    swap = remote(
        poly_all.at[c], poly_all.at[c], pair_s.at[1], pair_r.at[1], other_core
    )
    swap.start()
    remote(
        poly_all.at[1 - c], poly_all.at[1 - c], pair_s.at[1], pair_r.at[1], other_core
    ).wait_recv()
    for h in range(2):
        part_h = grad[:, h * HEAD_DIM : (h + 1) * HEAD_DIM]
        result = mmh(part_h, poly_all[h], NT)
        upd_v[:, h * HEAD_DIM : (h + 1) * HEAD_DIM] = result * (0.2 * D**0.5)
    upd_out = pltpu.make_async_copy(upd_v, upd_hbm, out_sem.at[3])
    upd_out.start()

    def drain(i, carry):
        for half in range(2):
            for kv in range(2):
                for way in range(2):
                    halo_copy(i, half, kv, way).wait_send()
                    far_copy(i, half, kv, way).wait_send()
        for slot in range(1, 4):
            att_copy(i, slot).wait_send()
        return carry

    lax.fori_loop(0, hc, drain, 0)
    for slot in range(1, 4):
        proj_copy(slot).wait_send()
    for i in range(hc):
        for d in range(1, nx if i % 2 == 0 else ny):
            first_copy(i, d).wait_send()
        for d in range(1, ny if i % 2 == 0 else nx):
            second_copy(i, d).wait_send()
        if i > 0:
            z_copy(i).wait_send()

    @pl.when(~stays)
    def _():
        z_copy(0).wait_send()

    pair.wait_send()
    swap.wait_send()
    for r in range(1, chips):
        g1_copy(r).wait_send()
        g2_copy(r).wait_send()
    for out in (dq_out, dk_out, dv_out, upd_out):
        out.wait()


def settle_kernel(*refs):
    count = (len(refs) - 2) // 3
    ins, outs, kept = refs[:count], refs[count : 2 * count], refs[2 * count : 3 * count]
    in_sem, out_sem = refs[-2:]
    loads = [
        pltpu.make_async_copy(ins[n], kept[n], in_sem.at[n]) for n in range(count)
    ]
    stores = [
        pltpu.make_async_copy(kept[n], outs[n], out_sem.at[n]) for n in range(count)
    ]
    for load in loads:
        load.start()
    for load, store in zip(loads, stores):
        load.wait()
        store.start()
    for store in stores:
        store.wait()


def settle(*arrays):
    anyspec = pl.BlockSpec(memory_space=pl.ANY)
    sems = pltpu.SemaphoreType.DMA((len(arrays),))
    return pl.pallas_call(
        settle_kernel,
        out_shape=tuple(jax.ShapeDtypeStruct(a.shape, a.dtype) for a in arrays),
        in_specs=[anyspec] * len(arrays),
        out_specs=(anyspec,) * len(arrays),
        scratch_shapes=[pltpu.VMEM(a.shape, a.dtype) for a in arrays] + [sems, sems],
        compiler_params=pltpu.CompilerParams(vmem_limit_bytes=60 * 2**20),
    )(*arrays)


def local(geo, query_tiles, key_tiles, value_tiles, attn_grad, proj_grad, neighbour):
    nz, ny, nx = geo
    seq = ny * nx * 2
    hc = nz // 2
    tile, width = query_tiles.shape[2:]
    depth = proj_grad.shape[3]
    hcols = depth // 2
    ccols = depth // seq
    cb = 2 * HEAD_DIM
    anyspec = pl.BlockSpec(memory_space=pl.ANY)
    chips = seq // 2
    rows = jax.ShapeDtypeStruct((tile, width), BF16)
    dma = pltpu.SemaphoreType.DMA
    halves = (2, 2, 2 * hc)
    square = (HEAD_DIM, HEAD_DIM)
    out = pl.pallas_call(
        functools.partial(kernel, geo),
        out_shape=(rows, rows, rows, jax.ShapeDtypeStruct((depth // seq, cb), F32)),
        in_specs=[pl.BlockSpec(memory_space=pltpu.SMEM)] + [anyspec] * 5,
        out_specs=(anyspec,) * 4,
        scratch_shapes=[pltpu.VMEM((tile, width), BF16)] * 7
        + [
            pltpu.VMEM((depth // seq, cb), F32),
            pltpu.VMEM(halves + (tile, cb), BF16),
            pltpu.VMEM((3, 2 * hc, tile, cb), BF16),
            pltpu.VMEM(halves + (tile, cb), BF16),
            pltpu.VMEM((tile, width), F32),
            pltpu.VMEM((tile, width), F32),
            pltpu.VMEM((4, tile, hcols), BF16),
            pltpu.VMEM((hcols, 4 * tile), BF16),
            pltpu.VMEM((hc, 4 * tile, cb), BF16),
            pltpu.VMEM((hc, ny, nx, ccols, cb), BF16),
            pltpu.VMEM((hc, ny, ny, ccols, cb), BF16),
            pltpu.VMEM((hc, ny, ccols, cb), BF16),
            pltpu.VMEM((hc, ny, ccols, cb), BF16),
            pltpu.VMEM((hc, ccols, cb), BF16),
            pltpu.VMEM((hc, ccols, cb), BF16),
            pltpu.VMEM((2,) + square, F32),
            pltpu.VMEM(square, F32),
            pltpu.VMEM(square, F32),
            pltpu.VMEM((chips, HEAD_DIM // chips, HEAD_DIM), F32),
            pltpu.VMEM(square, F32),
            pltpu.VMEM((2,) + square, F32),
            dma((5,)), dma((4,)),
            dma(halves), dma(halves), dma(halves), dma(halves),
            dma((4,)), dma((4,)),
            dma((hc, 4)), dma((hc, 4)),
            dma((hc, ny)), dma((hc, ny)), dma((hc, ny)), dma((hc, ny)),
            dma((hc,)), dma((hc,)),
            dma((2,)), dma((2,)),
            dma((chips,)), dma((chips,)), dma((chips,)), dma((chips,)),
        ],
        compiler_params=pltpu.CompilerParams(
            collective_id=0, has_side_effects=True, vmem_limit_bytes=60 * 2**20
        ),
    )(
        neighbour, query_tiles[0, 0], key_tiles[0, 0], value_tiles[0, 0],
        attn_grad[0, 0], proj_grad[0, 0],
    )
    dq, dk, dv, upd = settle(*out)
    return dq[None, None], dk[None, None], dv[None, None], upd.T


def solution(mesh):
    nz, seq = mesh.shape["dp"], mesh.shape["seq"]
    nx = 4 if seq == 32 else 2
    geo = (nz, seq // (2 * nx), nx)
    tiled = P("dp", "seq", None, None)
    return jax.shard_map(
        functools.partial(local, geo),
        mesh=mesh,
        in_specs=(tiled, tiled, tiled, tiled, tiled, P("dp", None)),
        out_specs=(tiled, tiled, tiled, P("dp", "seq")),
        check_vma=False,
    )
```

```python
import functools

import jax
import jax.numpy as jnp
from jax import lax
from jax.experimental import pallas as pl
from jax.experimental.pallas import tpu as pltpu
from jax.sharding import PartitionSpec as P

D = 3072
HEAD_DIM = 128
NS_STEPS = 5
MESH = pl.DeviceIdType.MESH
F32 = jnp.float32
BF16 = jnp.bfloat16
BEST = lax.Precision.HIGHEST

coeff_a = 3.4445
coeff_b = -4.775
coeff_c = 2.0315

NT = (((1,), (1,)), ((), ()))
NN = (((1,), (0,)), ((), ()))
TN = (((0,), (0,)), ((), ()))


def mm(a, b, dims):
    return lax.dot_general(a, b, dims, preferred_element_type=F32)


def mmh(a, b, dims=NN):
    return lax.dot_general(a, b, dims, precision=BEST, preferred_element_type=F32)


def head_grads(q, kk, vv, do):
    score_scale = HEAD_DIM ** (-0.5)
    scores = mm(q, kk, NT) * score_scale
    row_max = jnp.max(scores, axis=1, keepdims=True)
    exp_scores = jnp.exp(scores - row_max)
    weights = exp_scores / jnp.sum(exp_scores, axis=1, keepdims=True)
    weights_b = weights.astype(BF16)
    attended = mm(weights_b, vv, NN).astype(BF16)
    delta = jnp.sum(do.astype(F32) * attended.astype(F32), axis=1, keepdims=True)
    dweights = mm(do, vv, NT)
    dscore_b = (weights * (dweights - delta)).astype(BF16)
    dq = (mm(dscore_b, kk, NN) * score_scale).astype(BF16)
    dk = mm(dscore_b, q, TN) * score_scale
    dv = mm(weights_b, do, TN)
    return dq, dk, dv, attended


def kernel(
    geo,
    nb,
    q_hbm, k_hbm, v_hbm, do_hbm, proj_hbm,
    dq_v, dk_v, dv_v, upd_v,
    q_v, k_v, v_v, do_v,
    halo, far_out, far_in, own_k, own_v,
    proj_all, proj_t, att, part, rx1, sum1, rx2, sum2, rz,
    g_part, g_pair, g_mine, g_in, g_full, poly_all,
    in_sem,
    halo_s, halo_r, far_s, far_r,
    proj_s, proj_r,
    att_s, att_r, s1_s, s1_r, s2_s, s2_r, z_s, z_r,
    pair_s, pair_r, g1_s, g1_r, g2_s, g2_r,
    from_below, from_above, from_far,
):
    nz, ny, nx = geo
    seq = ny * nx * 2
    chips = ny * nx
    hc = nz // 2
    tile = q_v.shape[0]
    cb = 2 * HEAD_DIM
    hcols = proj_all.shape[2]
    ys = ny // 2
    ccols = hcols // chips
    z = lax.axis_index("dp")
    s = lax.axis_index("seq")
    c = lax.rem(s, 2)
    chip = s // 2
    x = lax.rem(chip, nx)
    y = chip // nx
    p = lax.rem(z, 2)
    zp = z // 2
    right = (z, lax.rem(s + 1, seq))
    left = (z, lax.rem(s + seq - 1, seq))
    other_core = (z, chip * 2 + 1 - c)

    def at(yy, xx, cc):
        return (z, (yy * nx + xx) * 2 + cc)

    def mate(cc):
        return (z + 1 - 2 * p, chip * 2 + cc)

    def y_off(d):
        return lax.rem(y + d, ny)

    def block_of(i, half):
        return 2 * lax.rem(zp + i, hc) + half

    def lanes(block):
        return pl.ds(pl.multiple_of(block * cb, cb), cb)

    def remote(src, dst, ss, rs, dev):
        return pltpu.make_async_remote_copy(
            src_ref=src, dst_ref=dst, send_sem=ss, recv_sem=rs,
            device_id=dev, device_id_type=MESH,
        )

    def half_cols(half):
        return pl.ds(pl.multiple_of(half * hcols, hcols), hcols)

    loads = [
        pltpu.make_async_copy(k_hbm, k_v, in_sem.at[1]),
        pltpu.make_async_copy(v_hbm, v_v, in_sem.at[2]),
        pltpu.make_async_copy(q_hbm, q_v, in_sem.at[0]),
        pltpu.make_async_copy(do_hbm, do_v, in_sem.at[3]),
        pltpu.make_async_copy(
            proj_hbm.at[:, half_cols(p)], proj_all.at[0], in_sem.at[4]
        ),
    ]
    for load in loads:
        load.start()

    barrier = pltpu.get_barrier_semaphore()

    def greet(dev):
        pl.semaphore_signal(barrier, inc=1, device_id=dev, device_id_type=MESH)

    def chip_off(r):
        return lax.rem(chip + r, chips)

    def owner(i):
        return (block_of(i, c), (((p * ys + y // 2) * nx) + x) * 2 + lax.rem(y, 2))

    stays = (c == p) & (p * ys + y // 2 == y) & (lax.rem(y, 2) == c)

    above = (lax.rem(z + 2, nz), s)
    below = (lax.rem(z + nz - 2, nz), s)
    for d in range(1, nx):
        greet(at(y, lax.rem(x + d, nx), c))
    for d in range(1, ny):
        greet(at(y_off(d), x, c))
    for dev in (other_core, mate(c), mate(1 - c), right, left, above, below):
        greet(dev)
    pl.semaphore_wait(barrier, nx + ny - 2 + 7)

    def halo_copy(i, half, kv, way):
        t = 2 * i + half
        src = (k_hbm, v_hbm)[kv].at[:, lanes(block_of(i, half))]
        return remote(
            src, halo.at[way, kv, t], halo_s.at[way, kv, t], halo_r.at[way, kv, t],
            (right, left)[way],
        )

    def start_halo(i, carry):
        for half in range(2):
            for kv in range(2):
                for way in range(2):
                    halo_copy(i, half, kv, way).start()
        return carry

    lax.fori_loop(0, hc, start_halo, 0)

    def proj_copy(slot):
        if slot == 3:
            src = proj_all.at[2]
        else:
            src = proj_hbm.at[:, half_cols(p if slot == 1 else 1 - p)]
        return remote(
            src, proj_all.at[slot], proj_s.at[slot], proj_r.at[slot],
            mate(c) if slot == 2 else other_core,
        )

    proj_copy(2).start()
    proj_copy(1).start()
    for load in loads:
        load.wait()

    def mask(condition):
        return jnp.where(condition, jnp.float32(1.0), jnp.float32(0.0))

    go_left = mask(nb[0, s] < s)
    go_right = 1.0 - go_left
    left_sends = mask(nb[0, jnp.maximum(s - 1, 0)] == s)
    right_sends = mask(nb[0, jnp.minimum(s + 1, seq - 1)] == s)

    def att_copy(i, slot):
        half = c if slot == 2 else 1 - c
        return remote(
            far_out.at[2, 2 * i + half], att.at[i, pl.ds(slot * tile, tile)],
            att_s.at[i, slot], att_r.at[i, slot],
            (None, other_core, mate(c), mate(1 - c))[slot],
        )

    def far_copy(i, half, kv, way):
        t = 2 * i + half
        return remote(
            far_out.at[kv, t], far_in.at[way, kv, t], far_s.at[way, kv, t],
            far_r.at[way, kv, t], (right, left)[way],
        )

    def start_far(i, half):
        for way in range(2):
            for kv in range(2):
                far_copy(i, half, kv, way).start()

    def turn(slot):
        turned = proj_all[slot].T
        for yy in range(ny):
            for xx in range(nx):
                start = (((yy // 2) * nx + xx) * 2 + yy % 2) * ccols
                place = (yy * nx + xx) * ccols
                proj_t[place : place + ccols, slot * tile : (slot + 1) * tile] = turned[
                    start : start + ccols
                ]

    def turn_all():
        turn(0)
        turn(2)
        for slot in (1, 3):
            proj_copy(slot).wait_recv()
            turn(slot)

    def first_copy(i, d):
        if i % 2 == 0:
            xx = lax.rem(x + d, nx)
            src, dev = part.at[i, :, xx], at(y, xx, c)
        else:
            src, dev = part.at[i, y_off(d)], at(y_off(d), x, c)
        return remote(src, rx1.at[i, d], s1_s.at[i, d], s1_r.at[i, d], dev)

    def second_copy(i, d):
        if i % 2 == 0:
            src, dev = sum1.at[i, y_off(d)], at(y_off(d), x, c)
        else:
            xx = lax.rem(x + d, nx)
            src, dev = sum1.at[i, xx], at(y, xx, c)
        return remote(src, rx2.at[i, d], s2_s.at[i, d], s2_r.at[i, d], dev)

    def z_copy(i):
        return remote(sum2.at[i], rz.at[i], z_s.at[i], z_r.at[i], owner(i))

    def product(i):
        for slot in range(1, 4):
            att_copy(i, slot).wait_recv()
        part[i] = mm(proj_t[...], att[i], NN).astype(BF16).reshape(part.shape[1:])
        for d in range(1, nx if i % 2 == 0 else ny):
            first_copy(i, d).start()

    early = min(2, hc - 1)
    far_early = min(1, hc - 1)

    def attend(i, carry):
        if early:

            @pl.when(i == hc - 1)
            def _():
                turn_all()
                for k in range(early):
                    product(k)

        for half in range(2):
            t = 2 * i + half
            block = block_of(i, half)
            for kv in range(2):
                for way in range(2):
                    halo_copy(i, half, kv, way).wait_recv()
            for h in range(2):
                inside = pl.ds(h * HEAD_DIM, HEAD_DIM)
                cols = pl.ds(
                    pl.multiple_of(block * cb + h * HEAD_DIM, HEAD_DIM), HEAD_DIM
                )

                def beside(kv):
                    from_left = halo[0, kv, t, :, inside].astype(F32) * go_left
                    from_right = halo[1, kv, t, :, inside].astype(F32) * go_right
                    return (from_left + from_right).astype(BF16)

                q = q_v[:, cols]
                do = do_v[:, cols]
                kk = jnp.concatenate([k_v[:, cols], beside(0)], 0)
                vv = jnp.concatenate([v_v[:, cols], beside(1)], 0)
                dq, dk, dv, attended = head_grads(q, kk, vv, do)
                dq_v[:, cols] = dq
                own_k[:, cols] = dk[:tile]
                own_v[:, cols] = dv[:tile]
                far_out[0, t, :, inside] = dk[tile:].astype(BF16)
                far_out[1, t, :, inside] = dv[tile:].astype(BF16)
                far_out[2, t, :, inside] = attended

            @pl.when(c == half)
            def _():
                att_copy(i, 2).start()
                att[i, pl.ds(0, tile)] = far_out[2, t]

            @pl.when(c != half)
            def _():
                att_copy(i, 3).start()
                att_copy(i, 1).start()

            if far_early:

                @pl.when(i < far_early)
                def _():
                    start_far(i, half)

        @pl.when(i == max(hc - 2, 0))
        def _():
            proj_copy(2).wait_recv()
            proj_copy(3).start()

        return carry

    lax.fori_loop(0, hc, attend, 0)

    if not early:
        turn_all()
    for i in range(early, hc):
        product(i)

    def tell(sem, dev):
        pl.semaphore_signal(sem, inc=1, device_id=dev, device_id_type=MESH)

    tell(from_below, above)
    tell(from_above, below)
    pl.semaphore_wait(from_below, 1)
    pl.semaphore_wait(from_above, 1)
    tell(from_far, above)
    for i in range(hc):
        total = (part[i, :, x] if i % 2 == 0 else part[i, y]).astype(F32)
        for d in range(1, nx if i % 2 == 0 else ny):
            first_copy(i, d).wait_recv()
            total = total + rx1[i, d].astype(F32)
        sum1[i] = total.astype(BF16)
        for d in range(1, ny if i % 2 == 0 else nx):
            second_copy(i, d).start()
    for i in range(hc):
        total = sum1[i, y if i % 2 == 0 else x].astype(F32)
        for d in range(1, ny if i % 2 == 0 else nx):
            second_copy(i, d).wait_recv()
            total = total + rx2[i, d].astype(F32)
        sum2[i] = total.astype(BF16)
        if i == 0:
            pl.semaphore_wait(from_far, 1)

            @pl.when(stays)
            def _():
                rz[0] = sum2[0]

            @pl.when(~stays)
            def _():
                z_copy(0).start()

        else:
            z_copy(i).start()

    def send_far(i, carry):
        for half in range(2):
            start_far(i, half)
        return carry

    lax.fori_loop(far_early, hc, send_far, 0)

    @pl.when(~stays)
    def _():
        z_copy(0).wait_recv()

    grad = rz[0].astype(F32)
    for i in range(1, hc):
        z_copy(i).wait_recv()
        grad = grad + rz[i].astype(F32)

    piece = HEAD_DIM // chips
    for h in range(2):
        part_h = grad[:, h * HEAD_DIM : (h + 1) * HEAD_DIM]
        g_part[h] = mmh(part_h, part_h, TN)
    pair = remote(
        g_part.at[1 - c], g_pair, pair_s.at[0], pair_r.at[0], other_core
    )
    pair.start()
    pair.wait_recv()
    g_mine[...] = g_part[c] + g_pair[...]

    def rows_of(index):
        return pl.ds(pl.multiple_of(index * piece, piece), piece)

    def g1_copy(r):
        there = chip_off(r)
        return remote(
            g_mine.at[rows_of(there)], g_in.at[r], g1_s.at[r], g1_r.at[r],
            (z, there * 2 + c),
        )

    def g2_copy(r):
        return remote(
            g_full.at[rows_of(chip)], g_full.at[rows_of(chip)], g2_s.at[r],
            g2_r.at[r], (z, chip_off(r) * 2 + c),
        )

    def g2_from(r):
        source = rows_of(lax.rem(chip + chips - r, chips))
        return remote(
            g_full.at[source], g_full.at[source], g2_s.at[r], g2_r.at[r], right
        )

    for r in range(1, chips):
        g1_copy(r).start()
    total = g_mine[rows_of(chip)]
    for r in range(1, chips):
        g1_copy(r).wait_recv()
        total = total + g_in[r]
    g_full[rows_of(chip)] = total
    for r in range(1, chips):
        g2_copy(r).start()

    def gather_far(i, carry):
        for half in range(2):
            t = 2 * i + half
            cols = lanes(block_of(i, half))
            for kv in range(2):
                for way in range(2):
                    far_copy(i, half, kv, way).wait_recv()
                out = (dk_v, dv_v)[kv]
                out[:, cols] = (
                    (own_k, own_v)[kv][:, cols]
                    + far_in[0, kv, t].astype(F32) * left_sends
                    + far_in[1, kv, t].astype(F32) * right_sends
                ).astype(BF16)
        return carry

    lax.fori_loop(0, hc, gather_far, 0)
    for r in range(1, chips):
        g2_from(r).wait_recv()

    row_id = lax.broadcasted_iota(jnp.int32, (HEAD_DIM, HEAD_DIM), 0)
    col_id = lax.broadcasted_iota(jnp.int32, (HEAD_DIM, HEAD_DIM), 1)
    eye = jnp.where(row_id == col_id, 1.0, 0.0).astype(F32)
    gram = g_full[...]
    trace = jnp.sum(jnp.sum(gram * eye, axis=1, keepdims=True), axis=0, keepdims=True)
    norm = jnp.sqrt(trace) + 1e-07
    gram = gram / norm / norm
    whole = None
    for turn_id in range(NS_STEPS):
        poly = coeff_a * eye + coeff_b * gram + coeff_c * mmh(gram, gram)
        if turn_id < NS_STEPS - 1:
            gram = mmh(mmh(poly, gram), poly)
        whole = poly if whole is None else mmh(poly, whole)
    poly_all[c] = whole / norm
    swap = remote(
        poly_all.at[c], poly_all.at[c], pair_s.at[1], pair_r.at[1], other_core
    )
    swap.start()
    remote(
        poly_all.at[1 - c], poly_all.at[1 - c], pair_s.at[1], pair_r.at[1], other_core
    ).wait_recv()
    for h in range(2):
        part_h = grad[:, h * HEAD_DIM : (h + 1) * HEAD_DIM]
        result = mmh(part_h, poly_all[h], NT)
        upd_v[:, h * HEAD_DIM : (h + 1) * HEAD_DIM] = result * (0.2 * D**0.5)
    def drain(i, carry):
        for half in range(2):
            for kv in range(2):
                for way in range(2):
                    halo_copy(i, half, kv, way).wait_send()
                    far_copy(i, half, kv, way).wait_send()
        for slot in range(1, 4):
            att_copy(i, slot).wait_send()
        return carry

    lax.fori_loop(0, hc, drain, 0)
    for slot in range(1, 4):
        proj_copy(slot).wait_send()
    for i in range(hc):
        for d in range(1, nx if i % 2 == 0 else ny):
            first_copy(i, d).wait_send()
        for d in range(1, ny if i % 2 == 0 else nx):
            second_copy(i, d).wait_send()
        if i > 0:
            z_copy(i).wait_send()

    @pl.when(~stays)
    def _():
        z_copy(0).wait_send()

    pair.wait_send()
    swap.wait_send()
    for r in range(1, chips):
        g1_copy(r).wait_send()
        g2_copy(r).wait_send()


def settle_kernel(*refs):
    count = len(refs) // 2
    sem = refs[-1]
    stores = [
        pltpu.make_async_copy(refs[n], refs[count + n], sem.at[n]) for n in range(count)
    ]
    for store in stores:
        store.start()
    for store in stores:
        store.wait()


def settle(*arrays):
    anyspec = pl.BlockSpec(memory_space=pl.ANY)
    sems = pltpu.SemaphoreType.DMA((len(arrays),))
    return pl.pallas_call(
        settle_kernel,
        out_shape=tuple(jax.ShapeDtypeStruct(a.shape, a.dtype) for a in arrays),
        in_specs=[anyspec] * len(arrays),
        out_specs=(anyspec,) * len(arrays),
        scratch_shapes=[sems],
        compiler_params=pltpu.CompilerParams(vmem_limit_bytes=8 * 2**20),
    )(*arrays)


def local(geo, query_tiles, key_tiles, value_tiles, attn_grad, proj_grad, neighbour):
    nz, ny, nx = geo
    seq = ny * nx * 2
    hc = nz // 2
    tile, width = query_tiles.shape[2:]
    depth = proj_grad.shape[3]
    hcols = depth // 2
    ccols = depth // seq
    cb = 2 * HEAD_DIM
    anyspec = pl.BlockSpec(memory_space=pl.ANY)
    chips = seq // 2
    rows = pltpu.VMEM((tile, width), BF16)
    dma = pltpu.SemaphoreType.DMA
    halves = (2, 2, 2 * hc)
    square = (HEAD_DIM, HEAD_DIM)
    out = pl.pallas_call(
        functools.partial(kernel, geo),
        out_shape=(rows, rows, rows, pltpu.VMEM((depth // seq, cb), F32)),
        in_specs=[pl.BlockSpec(memory_space=pltpu.SMEM)] + [anyspec] * 5,
        out_specs=(pl.BlockSpec(memory_space=pltpu.VMEM),) * 4,
        scratch_shapes=[pltpu.VMEM((tile, width), BF16)] * 4
        + [
            pltpu.VMEM(halves + (tile, cb), BF16),
            pltpu.VMEM((3, 2 * hc, tile, cb), BF16),
            pltpu.VMEM(halves + (tile, cb), BF16),
            pltpu.VMEM((tile, width), F32),
            pltpu.VMEM((tile, width), F32),
            pltpu.VMEM((4, tile, hcols), BF16),
            pltpu.VMEM((hcols, 4 * tile), BF16),
            pltpu.VMEM((hc, 4 * tile, cb), BF16),
            pltpu.VMEM((hc, ny, nx, ccols, cb), BF16),
            pltpu.VMEM((hc, ny, ny, ccols, cb), BF16),
            pltpu.VMEM((hc, ny, ccols, cb), BF16),
            pltpu.VMEM((hc, ny, ccols, cb), BF16),
            pltpu.VMEM((hc, ccols, cb), BF16),
            pltpu.VMEM((hc, ccols, cb), BF16),
            pltpu.VMEM((2,) + square, F32),
            pltpu.VMEM(square, F32),
            pltpu.VMEM(square, F32),
            pltpu.VMEM((chips, HEAD_DIM // chips, HEAD_DIM), F32),
            pltpu.VMEM(square, F32),
            pltpu.VMEM((2,) + square, F32),
            dma((5,)),
            dma(halves), dma(halves), dma(halves), dma(halves),
            dma((4,)), dma((4,)),
            dma((hc, 4)), dma((hc, 4)),
            dma((hc, ny)), dma((hc, ny)), dma((hc, ny)), dma((hc, ny)),
            dma((hc,)), dma((hc,)),
            dma((2,)), dma((2,)),
            dma((chips,)), dma((chips,)), dma((chips,)), dma((chips,)),
            pltpu.SemaphoreType.REGULAR, pltpu.SemaphoreType.REGULAR,
            pltpu.SemaphoreType.REGULAR,
        ],
        compiler_params=pltpu.CompilerParams(
            collective_id=0, has_side_effects=True, vmem_limit_bytes=62 * 2**20
        ),
    )(
        neighbour, query_tiles[0, 0], key_tiles[0, 0], value_tiles[0, 0],
        attn_grad[0, 0], proj_grad[0, 0],
    )
    dq, dk, dv, upd = settle(*out)
    return dq[None, None], dk[None, None], dv[None, None], upd.T


def solution(mesh):
    nz, seq = mesh.shape["dp"], mesh.shape["seq"]
    nx = 4 if seq == 32 else 2
    geo = (nz, seq // (2 * nx), nx)
    tiled = P("dp", "seq", None, None)
    return jax.shard_map(
        functools.partial(local, geo),
        mesh=mesh,
        in_specs=(tiled, tiled, tiled, tiled, tiled, P("dp", None)),
        out_specs=(tiled, tiled, tiled, P("dp", "seq")),
        check_vma=False,
    )
```

```python
import functools

import jax
import jax.numpy as jnp
from jax import lax
from jax.experimental import pallas as pl
from jax.experimental.pallas import tpu as pltpu
from jax.sharding import PartitionSpec as P

D = 3072
HEAD_DIM = 128
NS_STEPS = 5
MESH = pl.DeviceIdType.MESH
F32 = jnp.float32
BF16 = jnp.bfloat16
BEST = lax.Precision.HIGHEST

coeff_a = 3.4445
coeff_b = -4.775
coeff_c = 2.0315

NT = (((1,), (1,)), ((), ()))
NN = (((1,), (0,)), ((), ()))
TN = (((0,), (0,)), ((), ()))


def mm(a, b, dims):
    return lax.dot_general(a, b, dims, preferred_element_type=F32)


def mmh(a, b, dims=NN):
    return lax.dot_general(a, b, dims, precision=BEST, preferred_element_type=F32)


def head_grads(heads):
    score_scale = HEAD_DIM ** (-0.5)
    scores = [mm(q, kk, NT) for q, kk, vv, do in heads]
    dweights = [mm(do, vv, NT) for q, kk, vv, do in heads]
    row_max = [jnp.max(t, axis=1, keepdims=True) for t in scores]
    exp_scores = [jnp.exp((t - m) * score_scale) for t, m in zip(scores, row_max)]
    inverse = [1.0 / jnp.sum(t, axis=1, keepdims=True) for t in exp_scores]
    weights = [t * r for t, r in zip(exp_scores, inverse)]
    weights_b = [t.astype(BF16) for t in weights]
    attended = [
        mm(t, vv, NN).astype(BF16) for t, (q, kk, vv, do) in zip(weights_b, heads)
    ]
    delta = [
        jnp.sum(do.astype(F32) * t.astype(F32), axis=1, keepdims=True)
        for t, (q, kk, vv, do) in zip(attended, heads)
    ]
    dv = [mm(t, do, TN) for t, (q, kk, vv, do) in zip(weights_b, heads)]
    dscore_b = [
        (w * (dw - dl)).astype(BF16) for w, dw, dl in zip(weights, dweights, delta)
    ]
    dq = [
        (mm(t, kk, NN) * score_scale).astype(BF16)
        for t, (q, kk, vv, do) in zip(dscore_b, heads)
    ]
    dk = [mm(t, q, TN) * score_scale for t, (q, kk, vv, do) in zip(dscore_b, heads)]
    return list(zip(dq, dk, dv, attended))


def kernel(
    geo,
    nb,
    q_hbm, k_hbm, v_hbm, do_hbm, proj_hbm,
    dq_v, dk_v, dv_v, upd_v,
    q_v, k_v, v_v, do_v,
    halo, far_out, far_in, own_k, own_v,
    proj_all, proj_t, att, part, rx1, sum1, rx2, sum2, rz,
    g_part, g_pair, g_mine, g_in, g_full, poly_all,
    in_sem,
    halo_s, halo_r, far_s, far_r,
    proj_s, proj_r,
    att_s, att_r, s1_s, s1_r, s2_s, s2_r, z_s, z_r,
    pair_s, pair_r, g1_s, g1_r, g2_s, g2_r,
    from_below, from_above, from_far,
):
    nz, ny, nx = geo
    seq = ny * nx * 2
    chips = ny * nx
    hc = nz // 2
    tile = q_v.shape[0]
    cb = 2 * HEAD_DIM
    hcols = proj_all.shape[2]
    ys = ny // 2
    ccols = hcols // chips
    z = lax.axis_index("dp")
    s = lax.axis_index("seq")
    c = lax.rem(s, 2)
    chip = s // 2
    x = lax.rem(chip, nx)
    y = chip // nx
    p = lax.rem(z, 2)
    zp = z // 2
    right = (z, lax.rem(s + 1, seq))
    left = (z, lax.rem(s + seq - 1, seq))
    other_core = (z, chip * 2 + 1 - c)

    def at(yy, xx, cc):
        return (z, (yy * nx + xx) * 2 + cc)

    def mate(cc):
        return (z + 1 - 2 * p, chip * 2 + cc)

    def y_off(d):
        return lax.rem(y + d, ny)

    def block_of(i, half):
        return 2 * lax.rem(zp + i, hc) + half

    def lanes(block):
        return pl.ds(pl.multiple_of(block * cb, cb), cb)

    def remote(src, dst, ss, rs, dev):
        return pltpu.make_async_remote_copy(
            src_ref=src, dst_ref=dst, send_sem=ss, recv_sem=rs,
            device_id=dev, device_id_type=MESH,
        )

    def half_cols(half):
        return pl.ds(pl.multiple_of(half * hcols, hcols), hcols)

    loads = [
        pltpu.make_async_copy(k_hbm, k_v, in_sem.at[1]),
        pltpu.make_async_copy(v_hbm, v_v, in_sem.at[2]),
        pltpu.make_async_copy(q_hbm, q_v, in_sem.at[0]),
        pltpu.make_async_copy(do_hbm, do_v, in_sem.at[3]),
        pltpu.make_async_copy(
            proj_hbm.at[:, half_cols(p)], proj_all.at[0], in_sem.at[4]
        ),
    ]
    for load in loads:
        load.start()

    barrier = pltpu.get_barrier_semaphore()

    def greet(dev):
        pl.semaphore_signal(barrier, inc=1, device_id=dev, device_id_type=MESH)

    def chip_off(r):
        return lax.rem(chip + r, chips)

    def owner(i):
        return (block_of(i, c), (((p * ys + y // 2) * nx) + x) * 2 + lax.rem(y, 2))

    stays = (c == p) & (p * ys + y // 2 == y) & (lax.rem(y, 2) == c)

    above = (lax.rem(z + 2, nz), s)
    below = (lax.rem(z + nz - 2, nz), s)
    for d in range(1, nx):
        greet(at(y, lax.rem(x + d, nx), c))
    for d in range(1, ny):
        greet(at(y_off(d), x, c))
    for dev in (other_core, mate(c), mate(1 - c), right, left, above, below):
        greet(dev)
    pl.semaphore_wait(barrier, nx + ny - 2 + 7)

    def proj_copy(slot):
        if slot == 3:
            src = proj_all.at[2]
        else:
            src = proj_hbm.at[:, half_cols(p if slot == 1 else 1 - p)]
        return remote(
            src, proj_all.at[slot], proj_s.at[slot], proj_r.at[slot],
            mate(c) if slot == 2 else other_core,
        )

    proj_copy(2).start()
    proj_copy(1).start()
    def halo_copy(i, half, kv, way):
        t = 2 * i + half
        src = (k_hbm, v_hbm)[kv].at[:, lanes(block_of(i, half))]
        return remote(
            src, halo.at[way, kv, t], halo_s.at[way, kv, t], halo_r.at[way, kv, t],
            (right, left)[way],
        )

    def start_halo(i, carry):
        for half in range(2):
            for kv in range(2):
                for way in range(2):
                    halo_copy(i, half, kv, way).start()
        return carry

    lax.fori_loop(0, hc, start_halo, 0)

    for load in loads:
        load.wait()

    def mask(condition):
        return jnp.where(condition, jnp.float32(1.0), jnp.float32(0.0))

    go_left = mask(nb[0, s] < s)
    go_right = 1.0 - go_left
    left_sends = mask(nb[0, jnp.maximum(s - 1, 0)] == s)
    right_sends = mask(nb[0, jnp.minimum(s + 1, seq - 1)] == s)

    def att_copy(i, slot):
        half = c if slot == 2 else 1 - c
        return remote(
            far_out.at[2, 2 * i + half], att.at[i, pl.ds(slot * tile, tile)],
            att_s.at[i, slot], att_r.at[i, slot],
            (None, other_core, mate(c), mate(1 - c))[slot],
        )

    def far_copy(i, half, kv, way):
        t = 2 * i + half
        return remote(
            far_out.at[kv, t], far_in.at[way, kv, t], far_s.at[way, kv, t],
            far_r.at[way, kv, t], (right, left)[way],
        )

    def start_far(i, half):
        for way in range(2):
            for kv in range(2):
                far_copy(i, half, kv, way).start()

    def turn(slot):
        turned = proj_all[slot].T
        for yy in range(ny):
            for xx in range(nx):
                start = (((yy // 2) * nx + xx) * 2 + yy % 2) * ccols
                place = (yy * nx + xx) * ccols
                proj_t[place : place + ccols, slot * tile : (slot + 1) * tile] = turned[
                    start : start + ccols
                ]

    def turn_all():
        turn(2)
        proj_copy(3).wait_recv()
        turn(3)

    def first_copy(i, d):
        if i % 2 == 0:
            xx = lax.rem(x + d, nx)
            src, dev = part.at[i, :, xx], at(y, xx, c)
        else:
            src, dev = part.at[i, y_off(d)], at(y_off(d), x, c)
        return remote(src, rx1.at[i, d], s1_s.at[i, d], s1_r.at[i, d], dev)

    def second_copy(i, d):
        if i % 2 == 0:
            src, dev = sum1.at[i, y_off(d)], at(y_off(d), x, c)
        else:
            xx = lax.rem(x + d, nx)
            src, dev = sum1.at[i, xx], at(y, xx, c)
        return remote(src, rx2.at[i, d], s2_s.at[i, d], s2_r.at[i, d], dev)

    def z_copy(i):
        return remote(sum2.at[i], rz.at[i], z_s.at[i], z_r.at[i], owner(i))

    def product(i):
        for slot in range(1, 4):
            att_copy(i, slot).wait_recv()
        part[i] = mm(proj_t[...], att[i], NN).astype(BF16).reshape(part.shape[1:])
        for d in range(1, nx if i % 2 == 0 else ny):
            first_copy(i, d).start()

    early = min(2, hc - 1)
    far_early = min(1, hc - 1)

    def attend(i, carry):
        if early:

            @pl.when(i == hc - 1)
            def _():
                turn_all()
                for k in range(early):
                    product(k)

        for half in range(2):
            for kv in range(2):
                for way in range(2):
                    halo_copy(i, half, kv, way).wait_recv()

        def place(half, h):
            start = block_of(i, half) * cb + h * HEAD_DIM
            return pl.ds(pl.multiple_of(start, HEAD_DIM), HEAD_DIM)

        def beside(kv, half, h):
            t = 2 * i + half
            inside = pl.ds(h * HEAD_DIM, HEAD_DIM)
            from_left = halo[0, kv, t, :, inside].astype(F32) * go_left
            from_right = halo[1, kv, t, :, inside].astype(F32) * go_right
            return (from_left + from_right).astype(BF16)

        names = [(half, h) for half in range(2) for h in range(2)]
        heads = [
            (
                q_v[:, place(*n)],
                jnp.concatenate([k_v[:, place(*n)], beside(0, *n)], 0),
                jnp.concatenate([v_v[:, place(*n)], beside(1, *n)], 0),
                do_v[:, place(*n)],
            )
            for n in names
        ]
        for n, (dq, dk, dv, attended) in zip(names, head_grads(heads)):
            t = 2 * i + n[0]
            inside = pl.ds(n[1] * HEAD_DIM, HEAD_DIM)
            far_out[2, t, :, inside] = attended
            dq_v[:, place(*n)] = dq
            own_k[:, place(*n)] = dk[:tile]
            own_v[:, place(*n)] = dv[:tile]
            far_out[0, t, :, inside] = dk[tile:].astype(BF16)
            far_out[1, t, :, inside] = dv[tile:].astype(BF16)
        for half in range(2):
            t = 2 * i + half

            @pl.when(c == half)
            def _():
                att_copy(i, 2).start()
                att[i, pl.ds(0, tile)] = far_out[2, t]

            @pl.when(c != half)
            def _():
                att_copy(i, 3).start()
                att_copy(i, 1).start()

            if far_early:

                @pl.when(i < far_early)
                def _():
                    start_far(i, half)

        @pl.when(i == max(hc - 2, 0))
        def _():
            proj_copy(2).wait_recv()
            proj_copy(3).start()

        return carry

    turn(0)
    proj_copy(1).wait_recv()
    turn(1)
    lax.fori_loop(0, hc, attend, 0)

    if not early:
        turn_all()
    for i in range(early, hc):
        product(i)

    def tell(sem, dev):
        pl.semaphore_signal(sem, inc=1, device_id=dev, device_id_type=MESH)

    tell(from_below, above)
    tell(from_above, below)
    pl.semaphore_wait(from_below, 1)
    pl.semaphore_wait(from_above, 1)
    tell(from_far, above)
    for i in range(hc):
        total = (part[i, :, x] if i % 2 == 0 else part[i, y]).astype(F32)
        for d in range(1, nx if i % 2 == 0 else ny):
            first_copy(i, d).wait_recv()
            total = total + rx1[i, d].astype(F32)
        sum1[i] = total.astype(BF16)
        for d in range(1, ny if i % 2 == 0 else nx):
            second_copy(i, d).start()
    for i in range(hc):
        total = sum1[i, y if i % 2 == 0 else x].astype(F32)
        for d in range(1, ny if i % 2 == 0 else nx):
            second_copy(i, d).wait_recv()
            total = total + rx2[i, d].astype(F32)
        sum2[i] = total.astype(BF16)
        if i == 0:
            pl.semaphore_wait(from_far, 1)

            @pl.when(stays)
            def _():
                rz[0] = sum2[0]

            @pl.when(~stays)
            def _():
                z_copy(0).start()

        else:
            z_copy(i).start()

    @pl.when(~stays)
    def _():
        z_copy(0).wait_recv()

    grad = rz[0].astype(F32)
    for i in range(1, hc):
        z_copy(i).wait_recv()
        grad = grad + rz[i].astype(F32)

    piece = HEAD_DIM // chips
    for h in range(2):
        part_h = grad[:, h * HEAD_DIM : (h + 1) * HEAD_DIM]
        g_part[h] = mmh(part_h, part_h, TN)
    pair = remote(
        g_part.at[1 - c], g_pair, pair_s.at[0], pair_r.at[0], other_core
    )
    pair.start()
    pair.wait_recv()
    g_mine[...] = g_part[c] + g_pair[...]

    def rows_of(index):
        return pl.ds(pl.multiple_of(index * piece, piece), piece)

    def g1_copy(r):
        there = chip_off(r)
        return remote(
            g_mine.at[rows_of(there)], g_in.at[r], g1_s.at[r], g1_r.at[r],
            (z, there * 2 + c),
        )

    def g2_copy(r):
        return remote(
            g_full.at[rows_of(chip)], g_full.at[rows_of(chip)], g2_s.at[r],
            g2_r.at[r], (z, chip_off(r) * 2 + c),
        )

    def g2_from(r):
        source = rows_of(lax.rem(chip + chips - r, chips))
        return remote(
            g_full.at[source], g_full.at[source], g2_s.at[r], g2_r.at[r], right
        )

    for r in range(1, chips):
        g1_copy(r).start()
    total = g_mine[rows_of(chip)]
    for r in range(1, chips):
        g1_copy(r).wait_recv()
        total = total + g_in[r]
    g_full[rows_of(chip)] = total
    for r in range(1, chips):
        g2_copy(r).start()

    def send_far(i, carry):
        for half in range(2):
            start_far(i, half)
        return carry

    lax.fori_loop(far_early, hc, send_far, 0)

    for r in range(1, chips):
        g2_from(r).wait_recv()

    row_id = lax.broadcasted_iota(jnp.int32, (HEAD_DIM, HEAD_DIM), 0)
    col_id = lax.broadcasted_iota(jnp.int32, (HEAD_DIM, HEAD_DIM), 1)
    eye = jnp.where(row_id == col_id, 1.0, 0.0).astype(F32)
    gram = g_full[...]
    trace = jnp.sum(jnp.sum(gram * eye, axis=1, keepdims=True), axis=0, keepdims=True)
    norm = jnp.sqrt(trace) + 1e-07
    gram = gram / norm / norm
    whole = None
    for turn_id in range(NS_STEPS):
        poly = coeff_a * eye + coeff_b * gram + coeff_c * mmh(gram, gram)
        if turn_id < NS_STEPS - 1:
            gram = mmh(mmh(poly, gram), poly)
        whole = poly if whole is None else mmh(poly, whole)
    poly_all[c] = whole / norm
    swap = remote(
        poly_all.at[c], poly_all.at[c], pair_s.at[1], pair_r.at[1], other_core
    )
    swap.start()
    remote(
        poly_all.at[1 - c], poly_all.at[1 - c], pair_s.at[1], pair_r.at[1], other_core
    ).wait_recv()
    for h in range(2):
        part_h = grad[:, h * HEAD_DIM : (h + 1) * HEAD_DIM]
        result = mmh(part_h, poly_all[h], NT)
        upd_v[:, h * HEAD_DIM : (h + 1) * HEAD_DIM] = result * (0.2 * D**0.5)
    def gather_far(i, carry):
        for half in range(2):
            t = 2 * i + half
            cols = lanes(block_of(i, half))
            for kv in range(2):
                for way in range(2):
                    far_copy(i, half, kv, way).wait_recv()
                out = (dk_v, dv_v)[kv]
                out[:, cols] = (
                    (own_k, own_v)[kv][:, cols]
                    + far_in[0, kv, t].astype(F32) * left_sends
                    + far_in[1, kv, t].astype(F32) * right_sends
                ).astype(BF16)
        return carry

    lax.fori_loop(0, hc, gather_far, 0)
    def drain(i, carry):
        for half in range(2):
            for kv in range(2):
                for way in range(2):
                    halo_copy(i, half, kv, way).wait_send()
                    far_copy(i, half, kv, way).wait_send()
        for slot in range(1, 4):
            att_copy(i, slot).wait_send()
        return carry

    lax.fori_loop(0, hc, drain, 0)
    for slot in range(1, 4):
        proj_copy(slot).wait_send()
    for i in range(hc):
        for d in range(1, nx if i % 2 == 0 else ny):
            first_copy(i, d).wait_send()
        for d in range(1, ny if i % 2 == 0 else nx):
            second_copy(i, d).wait_send()
        if i > 0:
            z_copy(i).wait_send()

    @pl.when(~stays)
    def _():
        z_copy(0).wait_send()

    pair.wait_send()
    swap.wait_send()
    for r in range(1, chips):
        g1_copy(r).wait_send()
        g2_copy(r).wait_send()


def settle_kernel(*refs):
    count = len(refs) // 2
    sem = refs[-1]
    stores = [
        pltpu.make_async_copy(refs[n], refs[count + n], sem.at[n]) for n in range(count)
    ]
    for store in stores:
        store.start()
    for store in stores:
        store.wait()


def settle(*arrays):
    anyspec = pl.BlockSpec(memory_space=pl.ANY)
    sems = pltpu.SemaphoreType.DMA((len(arrays),))
    return pl.pallas_call(
        settle_kernel,
        out_shape=tuple(jax.ShapeDtypeStruct(a.shape, a.dtype) for a in arrays),
        in_specs=[anyspec] * len(arrays),
        out_specs=(anyspec,) * len(arrays),
        scratch_shapes=[sems],
        compiler_params=pltpu.CompilerParams(vmem_limit_bytes=8 * 2**20),
    )(*arrays)


def local(geo, query_tiles, key_tiles, value_tiles, attn_grad, proj_grad, neighbour):
    nz, ny, nx = geo
    seq = ny * nx * 2
    hc = nz // 2
    tile, width = query_tiles.shape[2:]
    depth = proj_grad.shape[3]
    hcols = depth // 2
    ccols = depth // seq
    cb = 2 * HEAD_DIM
    anyspec = pl.BlockSpec(memory_space=pl.ANY)
    chips = seq // 2
    rows = pltpu.VMEM((tile, width), BF16)
    dma = pltpu.SemaphoreType.DMA
    halves = (2, 2, 2 * hc)
    square = (HEAD_DIM, HEAD_DIM)
    out = pl.pallas_call(
        functools.partial(kernel, geo),
        out_shape=(rows, rows, rows, pltpu.VMEM((depth // seq, cb), F32)),
        in_specs=[pl.BlockSpec(memory_space=pltpu.SMEM)] + [anyspec] * 5,
        out_specs=(pl.BlockSpec(memory_space=pltpu.VMEM),) * 4,
        scratch_shapes=[pltpu.VMEM((tile, width), BF16)] * 4
        + [
            pltpu.VMEM(halves + (tile, cb), BF16),
            pltpu.VMEM((3, 2 * hc, tile, cb), BF16),
            pltpu.VMEM(halves + (tile, cb), BF16),
            pltpu.VMEM((tile, width), F32),
            pltpu.VMEM((tile, width), F32),
            pltpu.VMEM((4, tile, hcols), BF16),
            pltpu.VMEM((hcols, 4 * tile), BF16),
            pltpu.VMEM((hc, 4 * tile, cb), BF16),
            pltpu.VMEM((hc, ny, nx, ccols, cb), BF16),
            pltpu.VMEM((hc, ny, ny, ccols, cb), BF16),
            pltpu.VMEM((hc, ny, ccols, cb), BF16),
            pltpu.VMEM((hc, ny, ccols, cb), BF16),
            pltpu.VMEM((hc, ccols, cb), BF16),
            pltpu.VMEM((hc, ccols, cb), BF16),
            pltpu.VMEM((2,) + square, F32),
            pltpu.VMEM(square, F32),
            pltpu.VMEM(square, F32),
            pltpu.VMEM((chips, HEAD_DIM // chips, HEAD_DIM), F32),
            pltpu.VMEM(square, F32),
            pltpu.VMEM((2,) + square, F32),
            dma((5,)),
            dma(halves), dma(halves), dma(halves), dma(halves),
            dma((4,)), dma((4,)),
            dma((hc, 4)), dma((hc, 4)),
            dma((hc, ny)), dma((hc, ny)), dma((hc, ny)), dma((hc, ny)),
            dma((hc,)), dma((hc,)),
            dma((2,)), dma((2,)),
            dma((chips,)), dma((chips,)), dma((chips,)), dma((chips,)),
            pltpu.SemaphoreType.REGULAR, pltpu.SemaphoreType.REGULAR,
            pltpu.SemaphoreType.REGULAR,
        ],
        compiler_params=pltpu.CompilerParams(
            collective_id=0, has_side_effects=True, vmem_limit_bytes=62 * 2**20
        ),
    )(
        neighbour, query_tiles[0, 0], key_tiles[0, 0], value_tiles[0, 0],
        attn_grad[0, 0], proj_grad[0, 0],
    )
    dq, dk, dv, upd = settle(*out)
    return dq[None, None], dk[None, None], dv[None, None], upd.T


def solution(mesh):
    nz, seq = mesh.shape["dp"], mesh.shape["seq"]
    nx = 4 if seq == 32 else 2
    geo = (nz, seq // (2 * nx), nx)
    tiled = P("dp", "seq", None, None)
    return jax.shard_map(
        functools.partial(local, geo),
        mesh=mesh,
        in_specs=(tiled, tiled, tiled, tiled, tiled, P("dp", None)),
        out_specs=(tiled, tiled, tiled, P("dp", "seq")),
        check_vma=False,
    )
```

```python
import functools

import jax
import jax.numpy as jnp
from jax import lax
from jax.experimental import pallas as pl
from jax.experimental.pallas import tpu as pltpu
from jax.sharding import PartitionSpec as P

D = 3072
HEAD_DIM = 128
NS_STEPS = 5
MESH = pl.DeviceIdType.MESH
F32 = jnp.float32
BF16 = jnp.bfloat16
BEST = lax.Precision.HIGHEST

coeff_a = 3.4445
coeff_b = -4.775
coeff_c = 2.0315

NT = (((1,), (1,)), ((), ()))
NN = (((1,), (0,)), ((), ()))
TN = (((0,), (0,)), ((), ()))


def mm(a, b, dims):
    return lax.dot_general(a, b, dims, preferred_element_type=F32)


def mmh(a, b, dims=NN):
    return lax.dot_general(a, b, dims, precision=BEST, preferred_element_type=F32)


def head_grads(heads):
    score_scale = HEAD_DIM ** (-0.5)
    scores = [mm(q, kk, NT) for q, kk, vv, do in heads]
    dweights = [mm(do, vv, NT) for q, kk, vv, do in heads]
    row_max = [jnp.max(t, axis=1, keepdims=True) for t in scores]
    exp_scores = [jnp.exp((t - m) * score_scale) for t, m in zip(scores, row_max)]
    inverse = [1.0 / jnp.sum(t, axis=1, keepdims=True) for t in exp_scores]
    weights = [t * r for t, r in zip(exp_scores, inverse)]
    weights_b = [t.astype(BF16) for t in weights]
    attended = [
        mm(t, vv, NN).astype(BF16) for t, (q, kk, vv, do) in zip(weights_b, heads)
    ]
    delta = [
        jnp.sum(do.astype(F32) * t.astype(F32), axis=1, keepdims=True)
        for t, (q, kk, vv, do) in zip(attended, heads)
    ]
    dv = [mm(t, do, TN) for t, (q, kk, vv, do) in zip(weights_b, heads)]
    dscore_b = [
        (w * (dw - dl)).astype(BF16) for w, dw, dl in zip(weights, dweights, delta)
    ]
    dq = [
        (mm(t, kk, NN) * score_scale).astype(BF16)
        for t, (q, kk, vv, do) in zip(dscore_b, heads)
    ]
    dk = [mm(t, q, TN) * score_scale for t, (q, kk, vv, do) in zip(dscore_b, heads)]
    return list(zip(dq, dk, dv, attended))


def kernel(
    geo,
    nb,
    q_hbm, k_hbm, v_hbm, do_hbm, proj_hbm,
    dq_v, dk_v, dv_v, upd_v,
    q_v, k_v, v_v, do_v,
    halo, far_out, far_in, own_k, own_v,
    proj_all, proj_t, att, part, rx1, sum1, rx2, sum2, rz,
    g_part, g_pair, g_mine, g_in, g_full, poly_all,
    in_sem,
    halo_s, halo_r, far_s, far_r,
    proj_s, proj_r,
    att_s, att_r, s1_s, s1_r, s2_s, s2_r, z_s, z_r,
    pair_s, pair_r, g1_s, g1_r, g2_s, g2_r,
    from_below, from_above, from_far,
):
    nz, ny, nx = geo
    seq = ny * nx * 2
    chips = ny * nx
    hc = nz // 2
    tile = q_v.shape[0]
    cb = 2 * HEAD_DIM
    hcols = proj_all.shape[2]
    ys = ny // 2
    ccols = hcols // chips
    z = lax.axis_index("dp")
    s = lax.axis_index("seq")
    c = lax.rem(s, 2)
    chip = s // 2
    x = lax.rem(chip, nx)
    y = chip // nx
    p = lax.rem(z, 2)
    zp = z // 2
    right = (z, lax.rem(s + 1, seq))
    left = (z, lax.rem(s + seq - 1, seq))
    other_core = (z, chip * 2 + 1 - c)

    def at(yy, xx, cc):
        return (z, (yy * nx + xx) * 2 + cc)

    def mate(cc):
        return (z + 1 - 2 * p, chip * 2 + cc)

    def y_off(d):
        return lax.rem(y + d, ny)

    def block_of(i, half):
        return 2 * lax.rem(zp + i, hc) + half

    def lanes(block):
        return pl.ds(pl.multiple_of(block * cb, cb), cb)

    def remote(src, dst, ss, rs, dev):
        return pltpu.make_async_remote_copy(
            src_ref=src, dst_ref=dst, send_sem=ss, recv_sem=rs,
            device_id=dev, device_id_type=MESH,
        )

    def half_cols(half):
        return pl.ds(pl.multiple_of(half * hcols, hcols), hcols)

    loads = [
        pltpu.make_async_copy(k_hbm, k_v, in_sem.at[1]),
        pltpu.make_async_copy(v_hbm, v_v, in_sem.at[2]),
        pltpu.make_async_copy(q_hbm, q_v, in_sem.at[0]),
        pltpu.make_async_copy(do_hbm, do_v, in_sem.at[3]),
        pltpu.make_async_copy(
            proj_hbm.at[:, half_cols(p)], proj_all.at[0], in_sem.at[4]
        ),
    ]
    for load in loads:
        load.start()

    barrier = pltpu.get_barrier_semaphore()

    def greet(dev):
        pl.semaphore_signal(barrier, inc=1, device_id=dev, device_id_type=MESH)

    def chip_off(r):
        return lax.rem(chip + r, chips)

    def owner(i):
        return (block_of(i, c), (((p * ys + y // 2) * nx) + x) * 2 + lax.rem(y, 2))

    stays = (c == p) & (p * ys + y // 2 == y) & (lax.rem(y, 2) == c)

    above = (lax.rem(z + 2, nz), s)
    below = (lax.rem(z + nz - 2, nz), s)
    for d in range(1, nx):
        greet(at(y, lax.rem(x + d, nx), c))
    for d in range(1, ny):
        greet(at(y_off(d), x, c))
    for dev in (other_core, mate(c), mate(1 - c), right, left, above, below):
        greet(dev)
    pl.semaphore_wait(barrier, nx + ny - 2 + 7)

    def proj_copy(slot):
        if slot == 3:
            src = proj_all.at[2]
        else:
            src = proj_hbm.at[:, half_cols(p if slot == 1 else 1 - p)]
        return remote(
            src, proj_all.at[slot], proj_s.at[slot], proj_r.at[slot],
            mate(c) if slot == 2 else other_core,
        )

    proj_copy(2).start()
    proj_copy(1).start()
    def halo_copy(i, half, kv, way):
        t = 2 * i + half
        src = (k_hbm, v_hbm)[kv].at[:, lanes(block_of(i, half))]
        return remote(
            src, halo.at[way, kv, t], halo_s.at[way, kv, t], halo_r.at[way, kv, t],
            (right, left)[way],
        )

    def start_halo(i, carry):
        for half in range(2):
            for kv in range(2):
                for way in range(2):
                    halo_copy(i, half, kv, way).start()
        return carry

    lax.fori_loop(0, hc, start_halo, 0)

    for load in loads:
        load.wait()

    def mask(condition):
        return jnp.where(condition, jnp.float32(1.0), jnp.float32(0.0))

    go_left = mask(nb[0, s] < s)
    go_right = 1.0 - go_left
    left_sends = mask(nb[0, jnp.maximum(s - 1, 0)] == s)
    right_sends = mask(nb[0, jnp.minimum(s + 1, seq - 1)] == s)

    def att_copy(i, slot):
        half = c if slot == 2 else 1 - c
        return remote(
            far_out.at[2, 2 * i + half], att.at[i, pl.ds(slot * tile, tile)],
            att_s.at[i, slot], att_r.at[i, slot],
            (None, other_core, mate(c), mate(1 - c))[slot],
        )

    def far_copy(i, half, kv, way):
        t = 2 * i + half
        return remote(
            far_out.at[kv, t], far_in.at[way, kv, t], far_s.at[way, kv, t],
            far_r.at[way, kv, t], (right, left)[way],
        )

    def start_far(i, half):
        for way in range(2):
            for kv in range(2):
                far_copy(i, half, kv, way).start()

    def turn(slot):
        turned = proj_all[slot].T
        for yy in range(ny):
            for xx in range(nx):
                start = (((yy // 2) * nx + xx) * 2 + yy % 2) * ccols
                place = (yy * nx + xx) * ccols
                proj_t[place : place + ccols, slot * tile : (slot + 1) * tile] = turned[
                    start : start + ccols
                ]

    def turn_all():
        turn(2)
        proj_copy(3).wait_recv()
        turn(3)

    def first_copy(i, d):
        if i % 2 == 0:
            xx = lax.rem(x + d, nx)
            src, dev = part.at[i, :, xx], at(y, xx, c)
        else:
            src, dev = part.at[i, y_off(d)], at(y_off(d), x, c)
        return remote(src, rx1.at[i, d], s1_s.at[i, d], s1_r.at[i, d], dev)

    def second_copy(i, d):
        if i % 2 == 0:
            src, dev = sum1.at[i, y_off(d)], at(y_off(d), x, c)
        else:
            xx = lax.rem(x + d, nx)
            src, dev = sum1.at[i, xx], at(y, xx, c)
        return remote(src, rx2.at[i, d], s2_s.at[i, d], s2_r.at[i, d], dev)

    def z_copy(i):
        return remote(sum2.at[i], rz.at[i], z_s.at[i], z_r.at[i], owner(i))

    def product(i):
        for slot in range(1, 4):
            att_copy(i, slot).wait_recv()
        part[i] = mm(proj_t[...], att[i], NN).astype(BF16).reshape(part.shape[1:])
        for d in range(1, nx if i % 2 == 0 else ny):
            first_copy(i, d).start()

    early = min(2, hc - 1)
    far_early = min(1, hc - 1)

    def attend(i, carry):
        if early:

            @pl.when(i == hc - 1)
            def _():
                turn_all()
                for k in range(early):
                    product(k)

        for half in range(2):
            for kv in range(2):
                for way in range(2):
                    halo_copy(i, half, kv, way).wait_recv()

        def place(half, h):
            start = block_of(i, half) * cb + h * HEAD_DIM
            return pl.ds(pl.multiple_of(start, HEAD_DIM), HEAD_DIM)

        def beside(kv, half, h):
            t = 2 * i + half
            inside = pl.ds(h * HEAD_DIM, HEAD_DIM)
            from_left = halo[0, kv, t, :, inside].astype(F32) * go_left
            from_right = halo[1, kv, t, :, inside].astype(F32) * go_right
            return (from_left + from_right).astype(BF16)

        names = [(half, h) for half in range(2) for h in range(2)]
        heads = [
            (
                q_v[:, place(*n)],
                jnp.concatenate([k_v[:, place(*n)], beside(0, *n)], 0),
                jnp.concatenate([v_v[:, place(*n)], beside(1, *n)], 0),
                do_v[:, place(*n)],
            )
            for n in names
        ]
        for n, (dq, dk, dv, attended) in zip(names, head_grads(heads)):
            t = 2 * i + n[0]
            inside = pl.ds(n[1] * HEAD_DIM, HEAD_DIM)
            far_out[2, t, :, inside] = attended
            dq_v[:, place(*n)] = dq
            own_k[:, place(*n)] = dk[:tile]
            own_v[:, place(*n)] = dv[:tile]
            far_out[0, t, :, inside] = dk[tile:].astype(BF16)
            far_out[1, t, :, inside] = dv[tile:].astype(BF16)
        for half in range(2):
            t = 2 * i + half

            @pl.when(c == half)
            def _():
                att_copy(i, 2).start()
                att[i, pl.ds(0, tile)] = far_out[2, t]

            @pl.when(c != half)
            def _():
                att_copy(i, 3).start()
                att_copy(i, 1).start()

            if far_early:

                @pl.when(i < far_early)
                def _():
                    start_far(i, half)

        @pl.when(i == max(hc - 2, 0))
        def _():
            proj_copy(2).wait_recv()
            proj_copy(3).start()

        return carry

    turn(0)
    proj_copy(1).wait_recv()
    turn(1)
    lax.fori_loop(0, hc, attend, 0)

    if not early:
        turn_all()
    for i in range(early, hc):
        product(i)

    def tell(sem, dev):
        pl.semaphore_signal(sem, inc=1, device_id=dev, device_id_type=MESH)

    tell(from_below, above)
    tell(from_above, below)
    pl.semaphore_wait(from_below, 1)
    pl.semaphore_wait(from_above, 1)
    tell(from_far, above)
    for i in range(hc):
        total = (part[i, :, x] if i % 2 == 0 else part[i, y]).astype(F32)
        for d in range(1, nx if i % 2 == 0 else ny):
            first_copy(i, d).wait_recv()
            total = total + rx1[i, d].astype(F32)
        sum1[i] = total.astype(BF16)
        for d in range(1, ny if i % 2 == 0 else nx):
            second_copy(i, d).start()
    for i in range(hc):
        total = sum1[i, y if i % 2 == 0 else x].astype(F32)
        for d in range(1, ny if i % 2 == 0 else nx):
            second_copy(i, d).wait_recv()
            total = total + rx2[i, d].astype(F32)
        sum2[i] = total.astype(BF16)
        if i == 0:
            pl.semaphore_wait(from_far, 1)

            @pl.when(stays)
            def _():
                rz[0] = sum2[0]

            @pl.when(~stays)
            def _():
                z_copy(0).start()

        else:
            z_copy(i).start()

    @pl.when(~stays)
    def _():
        z_copy(0).wait_recv()

    grad = rz[0].astype(F32)
    for i in range(1, hc):
        z_copy(i).wait_recv()
        grad = grad + rz[i].astype(F32)

    piece = HEAD_DIM // chips
    first, second = grad[:, :HEAD_DIM], grad[:, HEAD_DIM:]
    mine = jnp.where(c == 0, first, second)
    theirs = jnp.where(c == 0, second, first)
    g_part[1 - c] = mmh(theirs, theirs, TN)
    pair = remote(
        g_part.at[1 - c], g_pair, pair_s.at[0], pair_r.at[0], other_core
    )
    pair.start()
    own_gram = mmh(mine, mine, TN)
    pair.wait_recv()
    g_mine[...] = own_gram + g_pair[...]

    def rows_of(index):
        return pl.ds(pl.multiple_of(index * piece, piece), piece)

    def g1_copy(r):
        there = chip_off(r)
        return remote(
            g_mine.at[rows_of(there)], g_in.at[r], g1_s.at[r], g1_r.at[r],
            (z, there * 2 + c),
        )

    def g2_copy(r):
        return remote(
            g_full.at[rows_of(chip)], g_full.at[rows_of(chip)], g2_s.at[r],
            g2_r.at[r], (z, chip_off(r) * 2 + c),
        )

    def g2_from(r):
        source = rows_of(lax.rem(chip + chips - r, chips))
        return remote(
            g_full.at[source], g_full.at[source], g2_s.at[r], g2_r.at[r], right
        )

    for r in range(1, chips):
        g1_copy(r).start()
    total = g_mine[rows_of(chip)]
    for r in range(1, chips):
        g1_copy(r).wait_recv()
        total = total + g_in[r]
    g_full[rows_of(chip)] = total
    for r in range(1, chips):
        g2_copy(r).start()

    def send_far(i, carry):
        for half in range(2):
            start_far(i, half)
        return carry

    lax.fori_loop(far_early, hc, send_far, 0)

    for r in range(1, chips):
        g2_from(r).wait_recv()

    row_id = lax.broadcasted_iota(jnp.int32, (HEAD_DIM, HEAD_DIM), 0)
    col_id = lax.broadcasted_iota(jnp.int32, (HEAD_DIM, HEAD_DIM), 1)
    eye = jnp.where(row_id == col_id, 1.0, 0.0).astype(F32)
    gram = g_full[...]
    trace = jnp.sum(jnp.sum(gram * eye, axis=1, keepdims=True), axis=0, keepdims=True)
    norm = jnp.sqrt(trace) + 1e-07
    gram = gram / norm / norm
    whole = None
    for turn_id in range(NS_STEPS):
        poly = coeff_a * eye + coeff_b * gram + coeff_c * mmh(gram, gram)
        if turn_id < NS_STEPS - 1:
            gram = mmh(mmh(poly, gram), poly)
        whole = poly if whole is None else mmh(poly, whole)
    poly_all[c] = whole / norm
    swap = remote(
        poly_all.at[c], poly_all.at[c], pair_s.at[1], pair_r.at[1], other_core
    )
    swap.start()

    def finish(head, part_h):
        result = mmh(part_h, poly_all[head], NT)
        place_h = pl.ds(pl.multiple_of(head * HEAD_DIM, HEAD_DIM), HEAD_DIM)
        upd_v[:, place_h] = result * (0.2 * D**0.5)

    finish(c, mine)
    remote(
        poly_all.at[1 - c], poly_all.at[1 - c], pair_s.at[1], pair_r.at[1], other_core
    ).wait_recv()
    finish(1 - c, theirs)

    def gather_far(i, carry):
        for half in range(2):
            t = 2 * i + half
            cols = lanes(block_of(i, half))
            for kv in range(2):
                for way in range(2):
                    far_copy(i, half, kv, way).wait_recv()
                out = (dk_v, dv_v)[kv]
                out[:, cols] = (
                    (own_k, own_v)[kv][:, cols]
                    + far_in[0, kv, t].astype(F32) * left_sends
                    + far_in[1, kv, t].astype(F32) * right_sends
                ).astype(BF16)
        return carry

    lax.fori_loop(0, hc, gather_far, 0)
    def drain(i, carry):
        for half in range(2):
            for kv in range(2):
                for way in range(2):
                    halo_copy(i, half, kv, way).wait_send()
                    far_copy(i, half, kv, way).wait_send()
        for slot in range(1, 4):
            att_copy(i, slot).wait_send()
        return carry

    lax.fori_loop(0, hc, drain, 0)
    for slot in range(1, 4):
        proj_copy(slot).wait_send()
    for i in range(hc):
        for d in range(1, nx if i % 2 == 0 else ny):
            first_copy(i, d).wait_send()
        for d in range(1, ny if i % 2 == 0 else nx):
            second_copy(i, d).wait_send()
        if i > 0:
            z_copy(i).wait_send()

    @pl.when(~stays)
    def _():
        z_copy(0).wait_send()

    pair.wait_send()
    swap.wait_send()
    for r in range(1, chips):
        g1_copy(r).wait_send()
        g2_copy(r).wait_send()


def settle_kernel(*refs):
    count = len(refs) // 2
    sem = refs[-1]
    stores = [
        pltpu.make_async_copy(refs[n], refs[count + n], sem.at[n]) for n in range(count)
    ]
    for store in stores:
        store.start()
    for store in stores:
        store.wait()


def settle(*arrays):
    anyspec = pl.BlockSpec(memory_space=pl.ANY)
    sems = pltpu.SemaphoreType.DMA((len(arrays),))
    return pl.pallas_call(
        settle_kernel,
        out_shape=tuple(jax.ShapeDtypeStruct(a.shape, a.dtype) for a in arrays),
        in_specs=[anyspec] * len(arrays),
        out_specs=(anyspec,) * len(arrays),
        scratch_shapes=[sems],
        compiler_params=pltpu.CompilerParams(vmem_limit_bytes=8 * 2**20),
    )(*arrays)


def local(geo, query_tiles, key_tiles, value_tiles, attn_grad, proj_grad, neighbour):
    nz, ny, nx = geo
    seq = ny * nx * 2
    hc = nz // 2
    tile, width = query_tiles.shape[2:]
    depth = proj_grad.shape[3]
    hcols = depth // 2
    ccols = depth // seq
    cb = 2 * HEAD_DIM
    anyspec = pl.BlockSpec(memory_space=pl.ANY)
    chips = seq // 2
    rows = pltpu.VMEM((tile, width), BF16)
    dma = pltpu.SemaphoreType.DMA
    halves = (2, 2, 2 * hc)
    square = (HEAD_DIM, HEAD_DIM)
    out = pl.pallas_call(
        functools.partial(kernel, geo),
        out_shape=(rows, rows, rows, pltpu.VMEM((depth // seq, cb), F32)),
        in_specs=[pl.BlockSpec(memory_space=pltpu.SMEM)] + [anyspec] * 5,
        out_specs=(pl.BlockSpec(memory_space=pltpu.VMEM),) * 4,
        scratch_shapes=[pltpu.VMEM((tile, width), BF16)] * 4
        + [
            pltpu.VMEM(halves + (tile, cb), BF16),
            pltpu.VMEM((3, 2 * hc, tile, cb), BF16),
            pltpu.VMEM(halves + (tile, cb), BF16),
            pltpu.VMEM((tile, width), F32),
            pltpu.VMEM((tile, width), F32),
            pltpu.VMEM((4, tile, hcols), BF16),
            pltpu.VMEM((hcols, 4 * tile), BF16),
            pltpu.VMEM((hc, 4 * tile, cb), BF16),
            pltpu.VMEM((hc, ny, nx, ccols, cb), BF16),
            pltpu.VMEM((hc, ny, ny, ccols, cb), BF16),
            pltpu.VMEM((hc, ny, ccols, cb), BF16),
            pltpu.VMEM((hc, ny, ccols, cb), BF16),
            pltpu.VMEM((hc, ccols, cb), BF16),
            pltpu.VMEM((hc, ccols, cb), BF16),
            pltpu.VMEM((2,) + square, F32),
            pltpu.VMEM(square, F32),
            pltpu.VMEM(square, F32),
            pltpu.VMEM((chips, HEAD_DIM // chips, HEAD_DIM), F32),
            pltpu.VMEM(square, F32),
            pltpu.VMEM((2,) + square, F32),
            dma((5,)),
            dma(halves), dma(halves), dma(halves), dma(halves),
            dma((4,)), dma((4,)),
            dma((hc, 4)), dma((hc, 4)),
            dma((hc, ny)), dma((hc, ny)), dma((hc, ny)), dma((hc, ny)),
            dma((hc,)), dma((hc,)),
            dma((2,)), dma((2,)),
            dma((chips,)), dma((chips,)), dma((chips,)), dma((chips,)),
            pltpu.SemaphoreType.REGULAR, pltpu.SemaphoreType.REGULAR,
            pltpu.SemaphoreType.REGULAR,
        ],
        compiler_params=pltpu.CompilerParams(
            collective_id=0, has_side_effects=True, vmem_limit_bytes=62 * 2**20
        ),
    )(
        neighbour, query_tiles[0, 0], key_tiles[0, 0], value_tiles[0, 0],
        attn_grad[0, 0], proj_grad[0, 0],
    )
    dq, dk, dv, upd = settle(*out)
    return dq[None, None], dk[None, None], dv[None, None], upd.T


def solution(mesh):
    nz, seq = mesh.shape["dp"], mesh.shape["seq"]
    nx = 4 if seq == 32 else 2
    geo = (nz, seq // (2 * nx), nx)
    tiled = P("dp", "seq", None, None)
    return jax.shard_map(
        functools.partial(local, geo),
        mesh=mesh,
        in_specs=(tiled, tiled, tiled, tiled, tiled, P("dp", None)),
        out_specs=(tiled, tiled, tiled, P("dp", "seq")),
        check_vma=False,
    )
```
